32 devices in a mesh: row: 8 (over z, x), col: 4 (over y, core).
Axes of the slice: x: 2, y: 2, z: 4, core: 2. Of those that a mesh axis runs over, the one named last changes fastest.
Arguments:
- tokens: bfloat16 [4096, 4096], P('row', 'col'), may hold values from -6 to 6
- gate_weight: bfloat16 [4096, 16384], P('row', 'col'), may hold values from -0.125 to 0.125
- up_weight: bfloat16 [4096, 16384], P('row', 'col'), may hold values from -0.125 to 0.125
- tile_mask: int32 [32, 128], P(None, 'col'), may hold values from 0 to 1, as said below
Outputs:
- hidden: bfloat16 [4096, 16384], P('row', 'col')
The draws below stay inside these ranges and needn't reach their ends.
Inputs may be any that keep to these rules, and one draw needn't show every extreme that they name: `tile_mask`: values are 0 or 1. In each aligned block of 4 x 32 tiles (tile rows r * 4 to (r + 1) * 4 - 1, tile columns c * 32 to (c + 1) * 32 - 1) at least 48 and at most 80 tiles are kept; some block keeps exactly 80.
All inputs are finite; a program needn't handle non-finite values.
Results may differ from the reference program's by a relative error of at most 0.001.
Values may be sent and summed in bfloat16 or wider, within the bound.
A program may use at most 128 MiB of HBM per device.

```python
import jax
import jax.numpy as jnp

D = 4096
F = 16384
TILE = 128
TOKENS = 4096
RB = 4
CB = 32
KEEP_MOST = 80
N_ROW = 8
N_COL = 4


def draw_tile_mask(key, part):
    key_count, key_chosen, key_score = jax.random.split(key, 3)
    tile_count = RB * CB
    fewest = 3 * tile_count // 8
    blocks = N_ROW * N_COL
    counts = jax.random.randint(key_count, (blocks,), fewest, KEEP_MOST + 1)
    chosen = jax.random.randint(key_chosen, (), 0, blocks)
    counts = jnp.where(jnp.arange(blocks) == chosen, KEEP_MOST, counts)
    scores = jax.random.randint(key_score, (blocks, tile_count), 0, 65536) * tile_count + jnp.arange(tile_count)[None, :]
    ordering = jnp.argsort(scores, axis=1, stable=True)
    ranking = jnp.argsort(ordering, axis=1, stable=True)
    kept_tiles = (ranking < counts[:, None]).astype(jnp.int32)
    kept_tiles = kept_tiles.reshape(N_ROW, N_COL, RB, CB).transpose(0, 2, 1, 3)
    return kept_tiles.reshape(N_ROW * RB, N_COL * CB)


def level_of(key, dims, cuts, low, largest):
    factor_of, own = 1.0, jax.random.fold_in(key, 6)
    for position, shards_of in cuts:
        steps = jnp.exp(jax.random.uniform(jax.random.fold_in(own, position), (shards_of,), jnp.float32, low / len(cuts), largest / len(cuts)))
        factor_of = factor_of * jnp.repeat(steps, dims[position] // shards_of).reshape([-1 if axis == position else 1 for axis in range(len(dims))])
    return factor_of


def gaussian(own_key, dims, deviation, most, shards=(), kind=jnp.bfloat16):
    factor_of = level_of(own_key, dims, shards, -0.22, 0.18) if shards else 1.0
    drawn = jax.random.normal(own_key, dims, jnp.float32) * deviation * factor_of
    return jnp.minimum(jnp.maximum(drawn, -most), most).astype(kind)


def setup_inputs(seed: int = 0) -> dict:
    key_of = jax.random.split(jax.random.key(seed), 5)
    tokens = gaussian(key_of[0], (TOKENS, D), 1.0, 6.0, ((0, 8), (1, 4)))
    gate_weight = gaussian(key_of[1], (D, F), (D // 2) ** -0.5, 0.125, ((0, 8), (1, 4)))
    up_weight = gaussian(key_of[2], (D, F), (D // 2) ** -0.5, 0.125, ((0, 8), (1, 4)))
    tile_mask = draw_tile_mask(jax.random.fold_in(key_of[4], 71), 0)
    return dict(tokens=tokens, gate_weight=gate_weight, up_weight=up_weight, tile_mask=tile_mask)


def spread_mask(tile_mask, dtype):
    return jnp.repeat(jnp.repeat(tile_mask, TILE, axis=0), TILE, axis=1).astype(dtype)


def reference(tokens, gate_weight, up_weight, tile_mask):
    keep_cells = spread_mask(tile_mask, gate_weight.dtype)
    gate_sum = jnp.dot(tokens, gate_weight * keep_cells, preferred_element_type=jnp.float32)
    up_sum = jnp.dot(tokens, up_weight * keep_cells, preferred_element_type=jnp.float32)
    return (jax.nn.silu(gate_sum) * up_sum).astype(jnp.bfloat16)
```

```python
import functools

import jax
import jax.numpy as jnp
from jax import lax
from jax.experimental import pallas as pl
from jax.experimental.pallas import tpu as pltpu
from jax.sharding import PartitionSpec as P

TILE = 128
VMEM_LIMIT = 60 * 1024 * 1024
MESH = pl.DeviceIdType.MESH


def pack_kernel(row_tiles, col_tiles, core_ref, mask_ref, gate_ref, up_ref, mine_ref, other_ref):
    core = core_ref[0]

    def column(j, slot):
        cols = pl.ds(pl.multiple_of(j * TILE, TILE), TILE)
        for i in range(row_tiles):
            kept = mask_ref[i * col_tiles + j]
            rows = pl.ds(i * TILE, TILE)

            @pl.when((kept == 1) & (core == 0))
            def _(slot=slot):
                mine_ref[slot] = gate_ref[rows, cols]
                other_ref[slot] = up_ref[rows, cols]

            @pl.when((kept == 1) & (core == 1))
            def _(slot=slot):
                mine_ref[slot] = up_ref[rows, cols]
                other_ref[slot] = gate_ref[rows, cols]

            slot = slot + kept
        return slot

    lax.fori_loop(0, col_tiles, column, jnp.int32(0))


def split(total, parts):
    parts = min(parts, total)
    edges = [total * n // parts for n in range(parts + 1)]
    return [(a, b - a) for a, b in zip(edges, edges[1:])]


def main_kernel(R, C, row_tiles, col_tiles, slots, codes_ref, tok_in, mine_ref, other_ref, out_ref, *scratch):
    NZ, NY = R // 2, C // 2
    rows, wide = tok_in.shape
    depth = row_tiles * TILE
    first = row_tiles * col_tiles // 2
    chunk_tiles = min(4, col_tiles // 4)
    width = chunk_tiles * TILE
    per_core = col_tiles // (4 * chunk_tiles)
    parts = [(0, *v) for v in split(first, 4)] + [(1, *v) for v in split(slots - first, 2)]
    nc = len(parts)
    firsts = [n for n in range(nc) if parts[n][0] == 0]
    lasts = [n for n in range(nc) if parts[n][0] == 1]

    scratch = list(scratch)
    take = lambda n: [scratch.pop(0) for _ in range(n)]
    own = take(2)
    far = [None] + [take(2) for _ in range(1, NZ)]
    across = [take(2) for _ in range(NZ)]
    tok, acc, dense, given, done = take(5)
    (w_send, w_recv, w_here, z_send, z_recv, x_send, x_recv, t_here, t_send, t_recv, ts_send, ts_recv,
     a_send, a_recv, o_send, os_send, o_recv, free) = take(18)

    r, c = lax.axis_index("row"), lax.axis_index("col")
    core = c % 2
    parity = (r // 2) % 2
    sibling = (r, c ^ 1)
    x_pair = (r ^ 1, c)
    owner = (c // 2) * 2 + parity

    def remote(src, dst, send, recv, device):
        return pltpu.make_async_remote_copy(
            src_ref=src, dst_ref=dst, send_sem=send, recv_sem=recv, device_id=device, device_id_type=MESH)

    partners = [sibling, x_pair, (r ^ 2, c ^ 1)]
    partners += [(r ^ (2 * d), c) for d in range(1, NZ)]
    partners += [(r, (c + 2 * s) % C) for s in range(1, NY)]
    barrier = pltpu.get_barrier_semaphore()
    for device in partners:
        pl.semaphore_signal(barrier, inc=1, device_id=device, device_id_type=MESH)
    pl.semaphore_wait(barrier, len(partners))

    def own_part(index, n):
        half, start, size = parts[n]
        return own[half].at[index, pl.ds(start, size)]

    def packed_part(ref, n):
        return ref.at[pl.ds(parts[n][1] + (first if parts[n][0] else 0), parts[n][2])]

    def piece_part(piece, n):
        half, start, size = parts[n]
        return piece[half].at[pl.ds(start, size)]

    def w_copy(n):
        return remote(packed_part(other_ref, n), own_part(core, n), w_send.at[n], w_recv.at[n], sibling)

    def w_arrival(n):
        return remote(packed_part(other_ref, n), own_part(1 - core, n), w_send.at[n], w_recv.at[n], sibling)

    def w_local(n):
        return pltpu.make_async_copy(packed_part(mine_ref, n), own_part(core, n), w_here.at[n])

    def z_copy(d, n):
        index = parity if d % 2 == 0 else 1 - parity
        return remote(own_part(index, n), piece_part(far[d], n), z_send.at[d, n], z_recv.at[d, n],
                      (r ^ (2 * d), c))

    def x_copy(d, n):
        src = own_part(parity, n) if d == 0 else piece_part(far[d], n)
        return remote(src, piece_part(across[d], n), x_send.at[d, n], x_recv.at[d, n], x_pair)

    def tok_place(group, col):
        return tok.at[pl.ds(group * rows, rows), pl.ds(pl.multiple_of(col * wide, TILE), wide)]

    def tok_copy(group, s):
        src = tok_in if group == 0 else tok_place(1, c)
        if s == 0:
            return remote(tok_in, tok_place(1, c), t_send.at[1, 0], t_recv.at[1, 0], (r ^ 2, c))
        return remote(src, tok_place(group, c), t_send.at[group, s], t_recv.at[group, s], (r, (c + 2 * s) % C))

    def tok_arrival(group, s):
        return remote(tok_in, tok_place(group, (c - 2 * s) % C), t_send.at[group, s], t_recv.at[group, s],
                      sibling)

    def tok_share(group, s):
        col = (c - 2 * s) % C
        src = tok_in if group == 0 and s == 0 else tok_place(group, col)
        return remote(src, tok_place(group, col), ts_send.at[group, s], ts_recv.at[group, s], sibling)

    def tok_shared(group, s):
        return remote(tok_in, tok_place(group, ((c ^ 1) - 2 * s) % C), ts_send.at[group, s],
                      ts_recv.at[group, s], sibling)

    tok_local = pltpu.make_async_copy(tok_in, tok_place(0, c), t_here)

    w_copy(0).start()
    w_local(0).start()
    tok_copy(1, 0).start()
    for n in range(1, nc):
        w_copy(n).start()
        w_local(n).start()
    for s in range(1, NY):
        tok_copy(0, s).start()
    cut = [d for d in range(2, NZ, 2)] + [d for d in range(3, NZ, 2)]
    order = [(d, n) for d in cut for n in firsts] + [(d, n) for d in cut for n in lasts]
    ahead = 2
    for n in range(nc):
        w_arrival(n).wait_recv()
        w_local(n).wait()
        if n < ahead:
            z_copy(1, n).start()
            z_copy(*order[n]).start()
        if n in firsts:
            x_copy(0, n).start()
    tok_share(0, 0).start()
    tok_local.start()

    def clear(n, carry):
        acc[n] = jnp.zeros(acc.shape[1:], acc.dtype)
        return carry

    lax.fori_loop(0, acc.shape[0], clear, 0)

    def job(piece, index, source, half, bounds):
        count, place = bounds

        def step(n, carry):
            chunk = half * 2 * per_core + place(n)
            for j in range(chunk_tiles):
                for i in range(row_tiles):
                    code = codes_ref[(source * row_tiles + i) * col_tiles + chunk * chunk_tiles + j]
                    low = jnp.minimum(jnp.maximum(code, 0), first - 1)
                    tile = piece[0][low] if index is None else piece[0][index, low]
                    zero = jnp.zeros_like(tile)
                    value = jnp.where(code >= 0, tile, zero)
                    if half:
                        high = jnp.maximum(code - first, 0)
                        late = piece[1][high] if index is None else piece[1][index, high]
                        value = jnp.where(code >= first, late, value)
                    dense[pl.ds(i * TILE, TILE), pl.ds(j * TILE, TILE)] = value
            lhs = tok[:, pl.ds(pl.multiple_of(source * depth, TILE), depth)]
            acc[chunk] += jnp.dot(lhs, dense[...], preferred_element_type=jnp.float32)
            return carry

        lax.fori_loop(0, count, step, 0)

    every = (2 * per_core, lambda n: n)
    theirs = (per_core, lambda n: (1 - core) * per_core + n)
    ours = (per_core, lambda n: core * per_core + n)

    def near_job(d, half, bounds=every):
        if d == 0:
            job(own, parity, r, half, bounds)
        else:
            job(far[d], None, r ^ (2 * d), half, bounds)

    arrived = set()

    def across_wait(d, ns):
        for n in ns:
            if (d, n) not in arrived:
                arrived.add((d, n))
                x_copy(d, n).wait_recv()

    def across_job(d, half, bounds=every):
        across_wait(d, firsts if half == 0 else range(nc))
        job(across[d], None, r ^ (2 * d) ^ 1, half, bounds)

    def sums_copy(half, i):
        chunk = half * 2 * per_core + (1 - core) * per_core + i
        return remote(acc.at[chunk], given.at[i], a_send.at[half, i], a_recv.at[half, i], sibling)

    def out_place(chunk):
        return out_ref.at[:, pl.ds(pl.multiple_of(chunk * width, TILE), width)]

    def done_part(half, i, group):
        return done.at[half * per_core + i, pl.ds(group * rows, rows)]

    def out_copy(half, i):
        chunk = half * 2 * per_core + core * per_core + i
        return remote(done_part(half, i, 1), out_place(chunk), o_send.at[half, i], o_recv.at[chunk], (r ^ 2, owner))

    def out_share(half, i):
        chunk = half * 2 * per_core + core * per_core + i
        return remote(done_part(half, i, 0), out_place(chunk), os_send.at[half, i], o_recv.at[chunk], sibling)

    def out_local(half, i):
        chunk = half * 2 * per_core + core * per_core + i
        return pltpu.make_async_copy(done_part(half, i, 0), out_place(chunk), o_recv.at[chunk])

    def finish(half, i):
        sums_copy(half, i).wait_recv()
        chunk = half * 2 * per_core + core * per_core + i
        block = min(128, rows)

        def rows_step(n, carry):
            here = pl.ds(pl.multiple_of(n * block, block), block)
            a, b = acc[chunk, here], given[i, here]
            gate = jnp.where(core == 0, a, b)
            up = jnp.where(core == 0, b, a)
            done[half * per_core + i, here] = (gate / (1.0 + jnp.exp(-gate)) * up).astype(done.dtype)
            return carry

        lax.fori_loop(rows // block, 2 * rows // block, rows_step, 0)
        out_copy(half, i).start()
        lax.fori_loop(0, rows // block, rows_step, 0)

        @pl.when(core == parity)
        def _():
            out_local(half, i).start()

        @pl.when(core != parity)
        def _():
            out_share(half, i).start()

    tok_arrival(1, 0).wait_recv()
    for s in range(1, NY):
        tok_copy(1, s).start()
    tok_share(1, 0).start()
    for s in range(1, NY):
        tok_arrival(0, s).wait_recv()
        tok_share(0, s).start()

    pair_order = firsts + lasts
    state = dict(pair=0)

    def pass_on(s):
        d, n = order[s]
        z_copy(d, n).wait_recv()
        x_copy(d, n).start()
        if s + ahead < len(order):
            z_copy(*order[s + ahead]).start()

    def pair_step():
        m = state["pair"]
        if m < nc:
            n = pair_order[m]
            z_copy(1, n).wait_recv()
            if n in firsts:
                x_copy(1, n).start()
            if m + ahead < nc:
                z_copy(1, pair_order[m + ahead]).start()
            state["pair"] = m + 1

    near_first = [("near", 0, 0), ("near", 0, 1), ("across", 0, 0)]
    ready = []
    head = len(firsts)
    total_first = len(cut) * head
    for s in range(total_first):
        pass_on(s)
        pair_step()
        if s == 0:
            for q in range(1, NY):
                tok_arrival(1, q).wait_recv()
                tok_share(1, q).start()
        if s == 1 or total_first == 1:
            tok_local.wait()
            for g in range(2):
                for q in range(NY):
                    tok_shared(g, q).wait_recv()
            ready += near_first
        if s + 1 == head:
            while state["pair"] < nc:
                pair_step()
            ready += [("near", 1, 0), ("near", 1, 1), ("across", 1, 0)]
        if (s + 1) % head == 0:
            ready += [("near", cut[s // head], 0)]
            if s // head:
                ready += [("across", cut[s // head - 1], 0)]
        if s + 3 == total_first:
            for n in lasts:
                x_copy(0, n).start()
                x_copy(1, n).start()
        budget = 2 if s + 1 < total_first else len(ready)
        while ready and budget:
            kind, d, half = ready.pop(0)
            (near_job if kind == "near" else across_job)(d, half)
            budget -= 1

    last = cut[-1]
    across_job(last, 0, theirs)
    for i in range(per_core):
        sums_copy(0, i).start()
    across_job(last, 0, ours)
    late = [("across", 0), ("across", 1)]
    for m in range(len(cut) * len(lasts)):
        pass_on(total_first + m)
        if m == 0:
            for i in range(per_core):
                finish(0, i)
                sums_copy(0, i).wait_send()
            pl.semaphore_signal(free, inc=1, device_id=sibling, device_id_type=MESH)
        e = m // len(lasts)
        if (m + 1) % len(lasts) == 0 and e + 1 < len(cut):
            late += [("near", cut[e])]
        if m % len(lasts) == 0 and e:
            late += [("across", cut[e - 1])]
        if m + 1 < len(cut) * len(lasts):
            for _ in range(min(2, len(late))):
                kind, d = late.pop(0)
                (near_job if kind == "near" else across_job)(d, 1)
    for kind, d in late:
        (near_job if kind == "near" else across_job)(d, 1)
    near_job(last, 1)
    across_job(last, 1, theirs)
    pl.semaphore_wait(free, 1)
    for i in range(per_core):
        sums_copy(1, i).start()
    across_job(last, 1, ours)
    for i in range(per_core):
        finish(1, i)

    for n in range(nc):
        w_copy(n).wait_send()
        for d in range(NZ):
            x_copy(d, n).wait_send()
            if d:
                z_copy(d, n).wait_send()
    for g in range(2):
        for s in range(NY):
            if g or s:
                tok_copy(g, s).wait_send()
            tok_share(g, s).wait_send()
    for i in range(per_core):
        sums_copy(1, i).wait_send()
        for half in range(2):
            out_copy(half, i).wait_send()

            @pl.when(core != parity)
            def _(half=half, i=i):
                out_share(half, i).wait_send()

    for chunk in range(4 * per_core):
        pltpu.make_async_copy(done_part(0, 0, 0), out_place(chunk), o_recv.at[chunk]).wait()


def solution(mesh):
    R, C = mesh.shape["row"], mesh.shape["col"]
    NZ, NY = R // 2, C // 2
    axes = ("row", "col")

    def on_device(tokens, gate_weight, up_weight, tile_mask):
        depth, cols = gate_weight.shape
        row_tiles, col_tiles = depth // TILE, cols // TILE
        tiles = row_tiles * col_tiles
        slots = 5 * tiles // 8
        rows = tokens.shape[0]
        r = lax.axis_index("row")
        core = lax.axis_index("col") % 2
        home = ((r // 2) % 2) == core

        mask_sib = lax.ppermute(tile_mask, axes, [(d, d ^ 1) for d in range(R * C)])
        smem = pl.BlockSpec(memory_space=pltpu.SMEM)
        vmem = pl.BlockSpec(memory_space=pltpu.VMEM)
        hbm = pl.BlockSpec(memory_space=pl.ANY)
        own_mask = lax.dynamic_slice_in_dim(tile_mask, r * row_tiles, row_tiles, 0).reshape(-1)
        piece = jax.ShapeDtypeStruct((slots, TILE, TILE), gate_weight.dtype)
        mine, other = pl.pallas_call(
            functools.partial(pack_kernel, row_tiles, col_tiles),
            out_shape=(piece, piece),
            in_specs=[smem, smem, vmem, vmem],
            out_specs=(vmem, vmem),
            compiler_params=pltpu.CompilerParams(vmem_limit_bytes=VMEM_LIMIT),
            name="pack",
        )(core.reshape(1).astype(jnp.int32), own_mask, gate_weight, up_weight)

        job_mask = jnp.where(home, tile_mask, mask_sib).reshape(R, row_tiles, col_tiles)
        place = jnp.arange(tiles)
        place = (place % col_tiles) * row_tiles + place // col_tiles
        upto = (place[None, :] <= place[:, None]).astype(jnp.int32)
        job_mask = job_mask.reshape(R, tiles)
        slot = jnp.sum(job_mask[:, None, :] * upto[None], axis=2) - 1
        codes = jnp.where(job_mask == 1, slot, -1).reshape(-1)

        first = tiles // 2
        chunk_tiles = min(4, col_tiles // 4)
        width = chunk_tiles * TILE
        per_core = col_tiles // (4 * chunk_tiles)
        nc = len(split(first, 4)) + len(split(slots - first, 2))
        bf16, f32 = jnp.bfloat16, jnp.float32
        pieces = [pltpu.VMEM((2, first, TILE, TILE), bf16), pltpu.VMEM((2, slots - first, TILE, TILE), bf16)]
        for _ in range(2 * NZ - 1):
            pieces += [pltpu.VMEM((first, TILE, TILE), bf16), pltpu.VMEM((slots - first, TILE, TILE), bf16)]
        sem = pltpu.SemaphoreType.DMA
        return pl.pallas_call(
            functools.partial(main_kernel, R, C, row_tiles, col_tiles, slots),
            out_shape=jax.ShapeDtypeStruct((rows, cols), bf16),
            in_specs=[smem, hbm, hbm, hbm],
            out_specs=hbm,
            scratch_shapes=pieces + [
                pltpu.VMEM((2 * rows, tokens.shape[1] * C), bf16),
                pltpu.VMEM((4 * per_core, 2 * rows, width), f32),
                pltpu.VMEM((depth, width), bf16),
                pltpu.VMEM((per_core, 2 * rows, width), f32),
                pltpu.VMEM((2 * per_core, 2 * rows, width), bf16),
                sem((nc,)), sem((nc,)), sem((nc,)),
                sem((NZ, nc)), sem((NZ, nc)), sem((NZ, nc)), sem((NZ, nc)),
                sem, sem((2, NY)), sem((2, NY)), sem((2, NY)), sem((2, NY)),
                sem((2, per_core)), sem((2, per_core)), sem((2, per_core)), sem((2, per_core)),
                sem((4 * per_core,)), pltpu.SemaphoreType.REGULAR,
            ],
            compiler_params=pltpu.CompilerParams(
                vmem_limit_bytes=VMEM_LIMIT, collective_id=0, has_side_effects=True),
            cost_estimate=pl.CostEstimate(
                flops=8 * rows * depth * R * cols // 2, bytes_accessed=rows * cols * 2, transcendentals=rows * cols),
            name="main",
        )(codes, tokens, mine, other)

    placed = (P("row", "col"), P("row", "col"), P("row", "col"), P(None, "col"))
    return jax.shard_map(
        on_device, mesh=mesh, in_specs=placed, out_specs=P("row", "col"), check_vma=False
    )
```

```python
import functools

import jax
import jax.numpy as jnp
from jax import lax
from jax.experimental import pallas as pl
from jax.experimental.pallas import tpu as pltpu
from jax.sharding import PartitionSpec as P

TILE = 128
VMEM_LIMIT = 60 * 1024 * 1024
FA, LB, AHEAD, BUDGET, LATE = 8, 4, 4, 1, 2
T1, T2, T3 = 0.5, 0.75, 1.0
MESH = pl.DeviceIdType.MESH


def copy_kernel(in_ref, out_ref):
    out_ref[...] = in_ref[...]


def split(total, parts):
    parts = min(parts, total)
    edges = [total * n // parts for n in range(parts + 1)]
    return [(a, b - a) for a, b in zip(edges, edges[1:])]


def main_kernel(R, C, row_tiles, col_tiles, slots, codes_ref, order_ref, tok_in, gate_in, up_in, out_ref, *scratch):
    NZ, NY = R // 2, C // 2
    rows, wide = tok_in.shape
    depth = row_tiles * TILE
    first = row_tiles * col_tiles // 2
    chunk_tiles = min(4, col_tiles // 4)
    width = chunk_tiles * TILE
    per_core = col_tiles // (4 * chunk_tiles)
    parts = [(0, *v) for v in split(first, FA)] + [(1, *v) for v in split(slots - first, LB)]
    nc = len(parts)
    firsts = [n for n in range(nc) if parts[n][0] == 0]
    lasts = [n for n in range(nc) if parts[n][0] == 1]

    scratch = list(scratch)
    take = lambda n: [scratch.pop(0) for _ in range(n)]
    own = take(2)
    other = take(2)
    far = [None] + [take(2) for _ in range(1, NZ)]
    across = [take(2) for _ in range(NZ)]
    tok, acc, dense, given, done = take(5)
    (w_send, w_recv, w_load, z_send, z_recv, x_send, x_recv, t_here, t_send, t_recv, ts_send, ts_recv,
     a_send, a_recv, o_send, os_send, o_recv, free) = take(18)

    r, c = lax.axis_index("row"), lax.axis_index("col")
    core = c % 2
    parity = (r // 2) % 2
    sibling = (r, c ^ 1)
    x_pair = (r ^ 1, c)
    owner = (c // 2) * 2 + parity

    def remote(src, dst, send, recv, device):
        return pltpu.make_async_remote_copy(
            src_ref=src, dst_ref=dst, send_sem=send, recv_sem=recv, device_id=device, device_id_type=MESH)

    loads = [pltpu.make_async_copy(ref, tok.at[pl.ds(n * depth, depth), pl.ds(0, col_tiles * TILE)], w_load.at[n])
             for n, ref in enumerate((gate_in, up_in))]
    for load in loads:
        load.start()
    for load in loads:
        load.wait()

    def pack(half, start, s):
        i, j = order_ref[r * slots + start + s], order_ref[(R + r) * slots + start + s]
        cols = pl.ds(j * TILE, TILE)
        mine_row = (core * row_tiles + i) * TILE
        other_row = ((1 - core) * row_tiles + i) * TILE
        own[half][core, s] = tok[pl.ds(mine_row, TILE), cols]
        other[half][s] = tok[pl.ds(other_row, TILE), cols]

    for half, start, stop in ((0, 0, first), (1, first, slots)):
        def pack_step(s, carry, half=half, start=start):
            pack(half, start, s)
            return carry

        lax.fori_loop(0, stop - start, pack_step, 0, unroll=min(4, stop - start))

    partners = [sibling, x_pair, (r ^ 2, c ^ 1)]
    partners += [(r ^ (2 * d), c) for d in range(1, NZ)]
    partners += [(r, (c + 2 * s) % C) for s in range(1, NY)]
    barrier = pltpu.get_barrier_semaphore()
    for device in partners:
        pl.semaphore_signal(barrier, inc=1, device_id=device, device_id_type=MESH)
    pl.semaphore_wait(barrier, len(partners))

    def own_part(index, n):
        half, start, size = parts[n]
        return own[half].at[index, pl.ds(start, size)]

    def piece_part(piece, n):
        half, start, size = parts[n]
        return piece[half].at[pl.ds(start, size)]

    def w_copy(n):
        return remote(piece_part(other, n), own_part(core, n), w_send.at[n], w_recv.at[n], sibling)

    def w_arrival(n):
        return remote(piece_part(other, n), own_part(1 - core, n), w_send.at[n], w_recv.at[n], sibling)

    def z_copy(d, n):
        index = parity if d % 2 == 0 else 1 - parity
        return remote(own_part(index, n), piece_part(far[d], n), z_send.at[d, n], z_recv.at[d, n],
                      (r ^ (2 * d), c))

    def x_copy(d, n):
        src = own_part(parity, n) if d == 0 else piece_part(far[d], n)
        return remote(src, piece_part(across[d], n), x_send.at[d, n], x_recv.at[d, n], x_pair)

    def tok_place(group, col):
        return tok.at[pl.ds(group * rows, rows), pl.ds(pl.multiple_of(col * wide, TILE), wide)]

    def tok_copy(group, s):
        src = tok_in if group == 0 else tok_place(1, c)
        if s == 0:
            return remote(tok_in, tok_place(1, c), t_send.at[1, 0], t_recv.at[1, 0], (r ^ 2, c))
        return remote(src, tok_place(group, c), t_send.at[group, s], t_recv.at[group, s], (r, (c + 2 * s) % C))

    def tok_arrival(group, s):
        return remote(tok_in, tok_place(group, (c - 2 * s) % C), t_send.at[group, s], t_recv.at[group, s],
                      sibling)

    def tok_share(group, s):
        col = (c - 2 * s) % C
        src = tok_in if group == 0 and s == 0 else tok_place(group, col)
        return remote(src, tok_place(group, col), ts_send.at[group, s], ts_recv.at[group, s], sibling)

    def tok_shared(group, s):
        return remote(tok_in, tok_place(group, ((c ^ 1) - 2 * s) % C), ts_send.at[group, s],
                      ts_recv.at[group, s], sibling)

    tok_local = pltpu.make_async_copy(tok_in, tok_place(0, c), t_here)

    w_copy(0).start()
    tok_copy(1, 0).start()
    for n in range(1, nc):
        w_copy(n).start()
    for s in range(1, NY):
        tok_copy(0, s).start()
    cut = [d for d in range(2, NZ, 2)] + [d for d in range(3, NZ, 2)]
    order = [(d, n) for d in cut for n in firsts] + [(d, n) for d in cut for n in lasts]
    ahead = AHEAD
    for n in range(nc):
        w_arrival(n).wait_recv()
        if n < ahead:
            z_copy(1, n).start()
            z_copy(*order[n]).start()
        x_copy(0, n).start()
    tok_share(0, 0).start()
    tok_local.start()

    def clear(n, carry):
        acc[n] = jnp.zeros(acc.shape[1:], acc.dtype)
        return carry

    lax.fori_loop(0, acc.shape[0], clear, 0)

    def job(piece, index, source, half, bounds):
        count, place, after = bounds

        def step(n, carry):
            chunk = half * 2 * per_core + place(n)
            for j in range(chunk_tiles):
                for i in range(row_tiles):
                    code = codes_ref[(source * row_tiles + i) * col_tiles + chunk * chunk_tiles + j]
                    low = jnp.minimum(jnp.maximum(code, 0), first - 1)
                    tile = piece[0][low] if index is None else piece[0][index, low]
                    zero = jnp.zeros_like(tile)
                    value = jnp.where(code >= 0, tile, zero)
                    if half:
                        high = jnp.maximum(code - first, 0)
                        late = piece[1][high] if index is None else piece[1][index, high]
                        value = jnp.where(code >= first, late, value)
                    dense[pl.ds(i * TILE, TILE), pl.ds(j * TILE, TILE)] = value
            lhs = tok[:, pl.ds(pl.multiple_of(source * depth, TILE), depth)]
            acc[chunk] += jnp.dot(lhs, dense[...], preferred_element_type=jnp.float32)
            if after:
                after(n)
            return carry

        lax.fori_loop(0, count, step, 0)

    def sums_copy(half, i, group):
        chunk = half * 2 * per_core + (1 - core) * per_core + i
        part = pl.ds(group * rows, rows)
        return remote(acc.at[chunk, part], given.at[i, part], a_send.at[half, i, group],
                      a_recv.at[half, i, group], sibling)

    every = (2 * per_core, lambda n: n, None)
    theirs = [(per_core, lambda n: (1 - core) * per_core + n, lambda n, h=h: sums_copy(h, n, 1).start())
              for h in range(2)]
    ours = (per_core, lambda n: core * per_core + n, None)

    def near_job(d, half, bounds=every):
        if d == 0:
            job(own, parity, r, half, bounds)
        else:
            job(far[d], None, r ^ (2 * d), half, bounds)

    arrived = set()

    def across_wait(d, ns):
        for n in ns:
            if (d, n) not in arrived:
                arrived.add((d, n))
                x_copy(d, n).wait_recv()

    def across_job(d, half, bounds=every):
        across_wait(d, firsts if half == 0 else range(nc))
        job(across[d], None, r ^ (2 * d) ^ 1, half, bounds)

    def out_place(chunk):
        return out_ref.at[:, pl.ds(pl.multiple_of(chunk * width, TILE), width)]

    def done_part(half, i, group):
        return done.at[half * per_core + i, pl.ds(group * rows, rows)]

    def out_copy(half, i):
        chunk = half * 2 * per_core + core * per_core + i
        return remote(done_part(half, i, 1), out_place(chunk), o_send.at[half, i], o_recv.at[chunk], (r ^ 2, owner))

    def out_share(half, i):
        chunk = half * 2 * per_core + core * per_core + i
        return remote(done_part(half, i, 0), out_place(chunk), os_send.at[half, i], o_recv.at[chunk], sibling)

    def out_local(half, i):
        chunk = half * 2 * per_core + core * per_core + i
        return pltpu.make_async_copy(done_part(half, i, 0), out_place(chunk), o_recv.at[chunk])

    def finish(half, i, group):
        sums_copy(half, i, group).wait_recv()
        chunk = half * 2 * per_core + core * per_core + i
        block = min(128, rows)

        def rows_step(n, carry):
            here = pl.ds(pl.multiple_of(group * rows + n * block, block), block)
            a, b = acc[chunk, here], given[i, here]
            gate = jnp.where(core == 0, a, b)
            up = jnp.where(core == 0, b, a)
            done[half * per_core + i, here] = (gate / (1.0 + jnp.exp(-gate)) * up).astype(done.dtype)
            return carry

        lax.fori_loop(0, rows // block, rows_step, 0)
        if group:
            out_copy(half, i).start()
        else:
            @pl.when(core == parity)
            def _():
                out_local(half, i).start()

            @pl.when(core != parity)
            def _():
                out_share(half, i).start()

    pair_order = firsts + lasts
    state = dict(pair=0)

    def pass_on(s):
        d, n = order[s]
        z_copy(d, n).wait_recv()
        x_copy(d, n).start()
        if s + ahead < len(order):
            z_copy(*order[s + ahead]).start()

    def pair_step():
        m = state["pair"]
        if m < nc:
            n = pair_order[m]
            z_copy(1, n).wait_recv()
            x_copy(1, n).start()
            if m + ahead < nc:
                z_copy(1, pair_order[m + ahead]).start()
            state["pair"] = m + 1

    def tokens_1():
        tok_arrival(1, 0).wait_recv()
        for s in range(1, NY):
            tok_copy(1, s).start()
        tok_share(1, 0).start()
        for s in range(1, NY):
            tok_arrival(0, s).wait_recv()
            tok_share(0, s).start()

    def tokens_2():
        for q in range(1, NY):
            tok_arrival(1, q).wait_recv()
            tok_share(1, q).start()

    def tokens_3():
        tok_local.wait()
        for g in range(2):
            for q in range(NY):
                tok_shared(g, q).wait_recv()

    head = len(firsts)
    total_first = len(cut) * head
    plan = {}

    def at(position, item):
        plan.setdefault(min(max(int(position * head) - 1, 0), total_first - 1), []).append(item)

    at(T1, tokens_1)
    at(T2, tokens_2)
    at(T3, tokens_3)
    for item in [("near", 0, 0), ("near", 0, 1), ("across", 0, 0), ("across", 0, 1), ("near", 1, 0)]:
        at(T3, item)
    for n, d in enumerate(cut):
        at(n + 1, ("near", d, 0))
        if n:
            at(n + 1, ("across", cut[n - 1], 0))
    at(1.5, ("across", 1, 0))
    at(1.5, ("near", 1, 1))
    ready = []
    for s in range(total_first):
        pass_on(s)
        pair_step()
        for item in plan.get(s, []):
            if callable(item):
                item()
            else:
                ready.append(item)
        if s + 1 == total_first:
            while state["pair"] < nc:
                pair_step()
        budget = BUDGET if s + 1 < total_first else len(ready)
        while ready and budget:
            kind, d, half = ready[0]
            if (kind, d, half) == ("near", 1, 1) and state["pair"] < nc:
                break
            ready.pop(0)
            (near_job if kind == "near" else across_job)(d, half)
            budget -= 1

    last = cut[-1]
    across_job(last, 0, theirs[0])
    across_job(last, 0, ours)
    for i in range(per_core):
        sums_copy(0, i, 0).start()
    late = [functools.partial(finish, 0, i, group) for group in (1, 0) for i in range(per_core)]

    def release():
        for group in range(2):
            for i in range(per_core):
                sums_copy(0, i, group).wait_send()
        pl.semaphore_signal(free, inc=1, device_id=sibling, device_id_type=MESH)

    late += [release, functools.partial(across_job, 1, 1)]
    steps = len(cut) * len(lasts)
    for m in range(steps):
        pass_on(total_first + m)
        e = m // len(lasts)
        if (m + 1) % len(lasts) == 0 and e + 1 < len(cut):
            late += [functools.partial(near_job, cut[e], 1)]
        if m % len(lasts) == 0 and e:
            late += [functools.partial(across_job, cut[e - 1], 1)]
        if m + 1 < steps:
            for _ in range(min(LATE, len(late))):
                late.pop(0)()
    for item in late:
        item()
    near_job(last, 1)
    pl.semaphore_wait(free, 1)
    across_job(last, 1, theirs[1])
    across_job(last, 1, ours)
    for i in range(per_core):
        sums_copy(1, i, 0).start()
    for group in (1, 0):
        for i in range(per_core):
            finish(1, i, group)

    for n in range(nc):
        w_copy(n).wait_send()
        for d in range(NZ):
            x_copy(d, n).wait_send()
            if d:
                z_copy(d, n).wait_send()
    for g in range(2):
        for s in range(NY):
            if g or s:
                tok_copy(g, s).wait_send()
            tok_share(g, s).wait_send()
    for i in range(per_core):
        for group in range(2):
            sums_copy(1, i, group).wait_send()
        for half in range(2):
            out_copy(half, i).wait_send()

            @pl.when(core != parity)
            def _(half=half, i=i):
                out_share(half, i).wait_send()

    for chunk in range(4 * per_core):
        pltpu.make_async_copy(done_part(0, 0, 0), out_place(chunk), o_recv.at[chunk]).wait()


def solution(mesh):
    R, C = mesh.shape["row"], mesh.shape["col"]
    NZ, NY = R // 2, C // 2
    axes = ("row", "col")

    def on_device(tokens, gate_weight, up_weight, tile_mask):
        depth, cols = gate_weight.shape
        row_tiles, col_tiles = depth // TILE, cols // TILE
        tiles = row_tiles * col_tiles
        slots = 5 * tiles // 8
        rows = tokens.shape[0]
        r = lax.axis_index("row")
        core = lax.axis_index("col") % 2
        home = ((r // 2) % 2) == core

        mask_sib = lax.ppermute(tile_mask, axes, [(d, d ^ 1) for d in range(R * C)])
        smem = pl.BlockSpec(memory_space=pltpu.SMEM)
        hbm = pl.BlockSpec(memory_space=pl.ANY)
        place = jnp.arange(tiles)
        place = (place % col_tiles) * row_tiles + place // col_tiles
        upto = (place[None, :] <= place[:, None]).astype(jnp.int32)

        def slot_codes(mask):
            mask = mask.reshape(R, tiles)
            return jnp.where(mask == 1, jnp.sum(mask[:, None, :] * upto[None], axis=2) - 1, -1)

        here = slot_codes(tile_mask)
        match = here[:, None, :] == jnp.arange(slots)[None, :, None]
        corner = jnp.stack([jnp.arange(tiles) // col_tiles, jnp.arange(tiles) % col_tiles])
        order = jnp.sum(jnp.where(match[None], corner[:, None, None, :], 0), axis=3).reshape(-1)
        codes = slot_codes(jnp.where(home, tile_mask, mask_sib)).reshape(-1)

        first = tiles // 2
        chunk_tiles = min(4, col_tiles // 4)
        width = chunk_tiles * TILE
        per_core = col_tiles // (4 * chunk_tiles)
        nc = len(split(first, FA)) + len(split(slots - first, LB))
        bf16, f32 = jnp.bfloat16, jnp.float32
        pieces = [pltpu.VMEM((2, first, TILE, TILE), bf16), pltpu.VMEM((2, slots - first, TILE, TILE), bf16)]
        for _ in range(2 * NZ):
            pieces += [pltpu.VMEM((first, TILE, TILE), bf16), pltpu.VMEM((slots - first, TILE, TILE), bf16)]
        sem = pltpu.SemaphoreType.DMA
        hidden = pl.pallas_call(
            functools.partial(main_kernel, R, C, row_tiles, col_tiles, slots),
            out_shape=jax.ShapeDtypeStruct((rows, cols), bf16),
            in_specs=[smem, smem, hbm, hbm, hbm],
            out_specs=hbm,
            scratch_shapes=pieces + [
                pltpu.VMEM((2 * rows, tokens.shape[1] * C), bf16),
                pltpu.VMEM((4 * per_core, 2 * rows, width), f32),
                pltpu.VMEM((depth, width), bf16),
                pltpu.VMEM((per_core, 2 * rows, width), f32),
                pltpu.VMEM((2 * per_core, 2 * rows, width), bf16),
                sem((nc,)), sem((nc,)), sem((2,)),
                sem((NZ, nc)), sem((NZ, nc)), sem((NZ, nc)), sem((NZ, nc)),
                sem, sem((2, NY)), sem((2, NY)), sem((2, NY)), sem((2, NY)),
                sem((2, per_core, 2)), sem((2, per_core, 2)), sem((2, per_core)), sem((2, per_core)),
                sem((4 * per_core,)), pltpu.SemaphoreType.REGULAR,
            ],
            compiler_params=pltpu.CompilerParams(
                vmem_limit_bytes=VMEM_LIMIT, collective_id=0, has_side_effects=True),
            cost_estimate=pl.CostEstimate(
                flops=8 * rows * depth * R * cols // 2, bytes_accessed=rows * cols * 2, transcendentals=rows * cols),
            name="main",
        )(codes, order, tokens, gate_weight, up_weight)
        part = pl.BlockSpec((rows // 4, cols), lambda n: (n, 0))
        return pl.pallas_call(
            copy_kernel,
            out_shape=jax.ShapeDtypeStruct((rows, cols), bf16),
            grid=(4,),
            in_specs=[part],
            out_specs=part,
            name="place",
        )(hidden)

    placed = (P("row", "col"), P("row", "col"), P("row", "col"), P(None, "col"))
    return jax.shard_map(
        on_device, mesh=mesh, in_specs=placed, out_specs=P("row", "col"), check_vma=False
    )
```

```python
import functools

import jax
import jax.numpy as jnp
from jax import lax
from jax.experimental import pallas as pl
from jax.experimental.pallas import tpu as pltpu
from jax.sharding import PartitionSpec as P

TILE = 128
VMEM_LIMIT = 63 * 1024 * 1024
AHEAD, LAG = 4, 3
T1, T2, T3 = 0.5, 0.75, 1.0
MESH = pl.DeviceIdType.MESH


def copy_kernel(in_ref, out_ref):
    out_ref[...] = in_ref[...]


def split(total, parts):
    parts = min(parts, total)
    edges = [total * n // parts for n in range(parts + 1)]
    return [(a, b - a) for a, b in zip(edges, edges[1:])]


def levels_of(row_tiles, col_tiles, slots):
    cuts = [col_tiles // 4, col_tiles // 2] if col_tiles >= 8 else [col_tiles // 2]
    return [(row_tiles * cols, cols) for cols in cuts] + [(slots, col_tiles)]


def parts_of(levels):
    parts, start = [], 0
    for n, (stop, _) in enumerate(levels):
        parts += [(n, *v) for v in split(stop - start, 4)]
        start = stop
    return parts


def main_kernel(R, C, row_tiles, col_tiles, slots, codes_ref, order_ref, tok_in, gate_in, up_in, out_ref, *scratch):
    NZ, NY = R // 2, C // 2
    rows, wide = tok_in.shape
    depth = row_tiles * TILE
    levels = levels_of(row_tiles, col_tiles, slots)
    L = len(levels)
    bottoms = [0] + [stop for stop, _ in levels[:-1]]
    chunk_tiles = min(4, levels[0][1] // 2)
    width = chunk_tiles * TILE
    lefts = [0] + [cols // chunk_tiles for _, cols in levels]
    per_core = [(b - a) // 2 for a, b in zip(lefts, lefts[1:])]
    parts = parts_of(levels)
    nc = len(parts)
    at_level = [[n for n in range(nc) if parts[n][0] == v] for v in range(L)]

    scratch = list(scratch)
    take = lambda n: [scratch.pop(0) for _ in range(n)]
    own = take(L)
    other = take(L)
    far = [None] + [take(L) for _ in range(1, NZ)]
    across = [take(L) for _ in range(NZ)]
    tok, acc, dense, given, done = take(5)
    (w_send, w_recv, w_load, z_send, z_recv, x_send, x_recv, t_here, t_send, t_recv, ts_send, ts_recv,
     a_send, a_recv, o_send, os_send, o_recv, free) = take(18)

    r, c = lax.axis_index("row"), lax.axis_index("col")
    core = c % 2
    parity = (r // 2) % 2
    sibling = (r, c ^ 1)
    x_pair = (r ^ 1, c)
    owner = (c // 2) * 2 + parity

    def remote(src, dst, send, recv, device):
        return pltpu.make_async_remote_copy(
            src_ref=src, dst_ref=dst, send_sem=send, recv_sem=recv, device_id=device, device_id_type=MESH)

    loads = [pltpu.make_async_copy(ref, tok.at[pl.ds(n * depth, depth), pl.ds(0, col_tiles * TILE)], w_load.at[n])
             for n, ref in enumerate((gate_in, up_in))]
    for load in loads:
        load.start()
    for load in loads:
        load.wait()

    for v in range(L):
        def pack_step(s, carry, v=v):
            n = r * slots + bottoms[v] + s
            i, j = order_ref[n], order_ref[R * slots + n]
            cols = pl.ds(j * TILE, TILE)
            mine_row = (core * row_tiles + i) * TILE
            other_row = ((1 - core) * row_tiles + i) * TILE
            own[v][core, s] = tok[pl.ds(mine_row, TILE), cols]
            other[v][s] = tok[pl.ds(other_row, TILE), cols]
            return carry

        count = levels[v][0] - bottoms[v]
        lax.fori_loop(0, count, pack_step, 0, unroll=min(4, count))

    partners = [sibling, x_pair, (r ^ 2, c ^ 1)]
    partners += [(r ^ (2 * d), c) for d in range(1, NZ)]
    partners += [(r, (c + 2 * s) % C) for s in range(1, NY)]
    barrier = pltpu.get_barrier_semaphore()
    for device in partners:
        pl.semaphore_signal(barrier, inc=1, device_id=device, device_id_type=MESH)
    pl.semaphore_wait(barrier, len(partners))

    def own_part(index, n):
        half, start, size = parts[n]
        return own[half].at[index, pl.ds(start, size)]

    def piece_part(piece, n):
        half, start, size = parts[n]
        return piece[half].at[pl.ds(start, size)]

    def w_copy(n):
        return remote(piece_part(other, n), own_part(core, n), w_send.at[n], w_recv.at[n], sibling)

    def w_arrival(n):
        return remote(piece_part(other, n), own_part(1 - core, n), w_send.at[n], w_recv.at[n], sibling)

    def z_copy(d, n):
        index = parity if d % 2 == 0 else 1 - parity
        return remote(own_part(index, n), piece_part(far[d], n), z_send.at[d, n], z_recv.at[d, n],
                      (r ^ (2 * d), c))

    def x_copy(d, n):
        src = own_part(parity, n) if d == 0 else piece_part(far[d], n)
        return remote(src, piece_part(across[d], n), x_send.at[d, n], x_recv.at[d, n], x_pair)

    def tok_place(group, col):
        return tok.at[pl.ds(group * rows, rows), pl.ds(pl.multiple_of(col * wide, TILE), wide)]

    def tok_copy(group, s):
        src = tok_in if group == 0 else tok_place(1, c)
        if s == 0:
            return remote(tok_in, tok_place(1, c), t_send.at[1, 0], t_recv.at[1, 0], (r ^ 2, c))
        return remote(src, tok_place(group, c), t_send.at[group, s], t_recv.at[group, s], (r, (c + 2 * s) % C))

    def tok_arrival(group, s):
        return remote(tok_in, tok_place(group, (c - 2 * s) % C), t_send.at[group, s], t_recv.at[group, s],
                      sibling)

    def tok_share(group, s):
        col = (c - 2 * s) % C
        src = tok_in if group == 0 and s == 0 else tok_place(group, col)
        return remote(src, tok_place(group, col), ts_send.at[group, s], ts_recv.at[group, s], sibling)

    def tok_shared(group, s):
        return remote(tok_in, tok_place(group, ((c ^ 1) - 2 * s) % C), ts_send.at[group, s],
                      ts_recv.at[group, s], sibling)

    tok_local = pltpu.make_async_copy(tok_in, tok_place(0, c), t_here)

    w_copy(0).start()
    tok_copy(1, 0).start()
    for n in range(1, nc):
        w_copy(n).start()
    for s in range(1, NY):
        tok_copy(0, s).start()
    cut = [d for d in range(2, NZ, 2)] + [d for d in range(3, NZ, 2)]
    order = [(d, n) for v in range(L) for d in cut for n in at_level[v]]
    ahead = AHEAD
    for n in range(nc):
        w_arrival(n).wait_recv()
        if n < ahead:
            z_copy(1, n).start()
            z_copy(*order[n]).start()
        x_copy(0, n).start()
    tok_share(0, 0).start()
    tok_local.start()

    def clear(n, carry):
        acc[n] = jnp.zeros(acc.shape[1:], acc.dtype)
        return carry

    lax.fori_loop(0, acc.shape[0], clear, 0)

    def job(piece, index, source, v, bounds):
        count, place, after = bounds

        def step(n, carry):
            chunk = place(n)
            for j in range(chunk_tiles):
                for i in range(row_tiles):
                    code = codes_ref[(source * row_tiles + i) * col_tiles + chunk * chunk_tiles + j]
                    value = None
                    for u in range(v + 1):
                        size = levels[u][0] - bottoms[u]
                        slot = jnp.minimum(jnp.maximum(code - bottoms[u], 0), size - 1)
                        tile = piece[u][slot] if index is None else piece[u][index, slot]
                        value = jnp.where(code >= bottoms[u], tile, jnp.zeros_like(tile) if value is None else value)
                    dense[pl.ds(i * TILE, TILE), pl.ds(j * TILE, TILE)] = value
            lhs = tok[:, pl.ds(pl.multiple_of(source * depth, TILE), depth)]
            acc[chunk] += jnp.dot(lhs, dense[...], preferred_element_type=jnp.float32)
            if after:
                after(n)
            return carry

        lax.fori_loop(0, count, step, 0)

    def our_chunk(v, i):
        return lefts[v] + core * per_core[v] + i

    def their_chunk(v, i):
        return lefts[v] + (1 - core) * per_core[v] + i

    def sums_copy(v, i, group):
        part = pl.ds(group * rows, rows)
        return remote(acc.at[their_chunk(v, i), part], given.at[i, part], a_send.at[v, i, group],
                      a_recv.at[v, i, group], sibling)

    every = [(2 * per_core[v], lambda n, v=v: lefts[v] + n, None) for v in range(L)]
    theirs = [(per_core[v], functools.partial(their_chunk, v), None) for v in range(L)]
    sent = [(per_core[v], functools.partial(their_chunk, v), lambda n, v=v: sums_copy(v, n, 1).start())
            for v in range(L)]
    ours = [(per_core[v], functools.partial(our_chunk, v), None) for v in range(L)]

    def near_job(d, v, bounds=every):
        if d == 0:
            job(own, parity, r, v, bounds[v])
        else:
            job(far[d], None, r ^ (2 * d), v, bounds[v])

    arrived = set()

    def across_job(d, v, bounds=every):
        for n in range(nc):
            if parts[n][0] <= v and (d, n) not in arrived:
                arrived.add((d, n))
                x_copy(d, n).wait_recv()
        job(across[d], None, r ^ (2 * d) ^ 1, v, bounds[v])

    def out_place(chunk):
        return out_ref.at[:, pl.ds(pl.multiple_of(chunk * width, TILE), width)]

    def done_part(v, i, group):
        return done.at[sum(per_core[:v]) + i, pl.ds(group * rows, rows)]

    def out_copy(v, i):
        return remote(done_part(v, i, 1), out_place(our_chunk(v, i)), o_send.at[sum(per_core[:v]) + i],
                      o_recv.at[our_chunk(v, i)], (r ^ 2, owner))

    def out_share(v, i):
        return remote(done_part(v, i, 0), out_place(our_chunk(v, i)), os_send.at[sum(per_core[:v]) + i],
                      o_recv.at[our_chunk(v, i)], sibling)

    def out_local(v, i):
        return pltpu.make_async_copy(done_part(v, i, 0), out_place(our_chunk(v, i)), o_recv.at[our_chunk(v, i)])

    def finish(v, i, group):
        sums_copy(v, i, group).wait_recv()
        chunk = our_chunk(v, i)
        block = min(128, rows)

        def rows_step(n, carry):
            here = pl.ds(pl.multiple_of(group * rows + n * block, block), block)
            a, b = acc[chunk, here], given[i, here]
            gate = jnp.where(core == 0, a, b)
            up = jnp.where(core == 0, b, a)
            done[sum(per_core[:v]) + i, here] = (gate / (1.0 + jnp.exp(-gate)) * up).astype(done.dtype)
            return carry

        lax.fori_loop(0, rows // block, rows_step, 0)
        if group:
            out_copy(v, i).start()
        else:
            @pl.when(core == parity)
            def _():
                out_local(v, i).start()

            @pl.when(core != parity)
            def _():
                out_share(v, i).start()

    state = dict(pair=0)
    later = []

    def pass_on(s):
        d, n = order[s]
        z_copy(d, n).wait_recv()
        x_copy(d, n).start()
        if s + ahead < len(order):
            z_copy(*order[s + ahead]).start()

    def pair_step():
        n = state["pair"]
        if n < nc:
            z_copy(1, n).wait_recv()
            if n in at_level[-1]:
                later.append((1, n))
            else:
                x_copy(1, n).start()
            if n + ahead < nc:
                z_copy(1, n + ahead).start()
            state["pair"] = n + 1

    def tokens_1():
        tok_arrival(1, 0).wait_recv()
        for s in range(1, NY):
            tok_copy(1, s).start()
        tok_share(1, 0).start()
        for s in range(1, NY):
            tok_arrival(0, s).wait_recv()
            tok_share(0, s).start()

    def tokens_2():
        for q in range(1, NY):
            tok_arrival(1, q).wait_recv()
            tok_share(1, q).start()

    def tokens_3():
        tok_local.wait()
        for g in range(2):
            for q in range(NY):
                tok_shared(g, q).wait_recv()

    steps = len(order)
    starts = [order.index((cut[0], at_level[v][0])) for v in range(L)]
    spread = starts[1] if L > 2 else starts[1] // 2
    head = len(at_level[0]) * len(cut)
    last = cut[-1]
    queue = []

    def at(step, cost, item):
        queue.append((max(step, 0), len(queue), cost, item))

    at(int(T1 * head) - 1, 0, tokens_1)
    at(int(T2 * head) - 1, 0, tokens_2)
    ready = int(T3 * head) - 1
    at(ready, 0, tokens_3)
    for v in range(L):
        there = {d: order.index((d, at_level[v][-1])) for d in cut}
        cost = 2 * per_core[v]
        at(max(ready, starts[max(v - 1, 0)]), cost, functools.partial(near_job, 0, v))
        at(max(ready, at_level[v][-1]), cost, functools.partial(near_job, 1, v))
        if v == L - 1:
            own_there = pair_there = starts[-1] + 1
        else:
            own_there = spread + at_level[v][-1] - at_level[1][0] + LAG if v else 0
            pair_there = at_level[v][-1] + LAG
        at(max(ready, own_there), cost, functools.partial(across_job, 0, v))
        at(max(ready, pair_there), cost, functools.partial(across_job, 1, v))
        for d in cut:
            final = v == L - 1 and d == last
            if not final:
                at(max(ready, there[d]), cost, functools.partial(near_job, d, v))
            if d != last:
                at(max(ready, there[d] + LAG), cost, functools.partial(across_job, d, v))

        def send_sums(v=v):
            if v:
                pl.semaphore_wait(free, 1)
            if v == L - 1:
                near_job(last, v, theirs)
            across_job(last, v, sent)
            if v == L - 1:
                near_job(last, v, ours)
            across_job(last, v, ours)
            for i in range(per_core[v]):
                sums_copy(v, i, 0).start()

        when = max(ready, there[last] + LAG) if v < L - 1 else steps
        at(when, cost, send_sums)
        for group in (1, 0):
            for i in range(per_core[v]):
                at(when + 1, 2, functools.partial(finish, v, i, group))

        def release(v=v):
            for group in range(2):
                for i in range(per_core[v]):
                    sums_copy(v, i, group).wait_send()
            if v < L - 1:
                pl.semaphore_signal(free, inc=1, device_id=sibling, device_id_type=MESH)

        at(when + 1, 0, release)

    queue.sort(key=lambda entry: entry[:2])
    for s in range(steps):
        pass_on(s)
        pair_step()
        if s >= spread:
            for _ in range(min(len(later), 1 if later and parts[later[0][1]][0] < L - 1 else 2)):
                x_copy(*later.pop(0)).start()
        if s + 1 == starts[-1]:
            while state["pair"] < nc:
                pair_step()
            while later:
                x_copy(*later.pop(0)).start()
        budget = 6 if s < starts[-1] else 4
        while queue and queue[0][0] <= s and budget > 0:
            _, _, cost, item = queue.pop(0)
            item()
            budget -= cost
    for entry in queue:
        entry[3]()

    for n in range(nc):
        w_copy(n).wait_send()
        for d in range(NZ):
            x_copy(d, n).wait_send()
            if d:
                z_copy(d, n).wait_send()
    for g in range(2):
        for s in range(NY):
            if g or s:
                tok_copy(g, s).wait_send()
            tok_share(g, s).wait_send()
    for v in range(L):
        for i in range(per_core[v]):
            out_copy(v, i).wait_send()

            @pl.when(core != parity)
            def _(v=v, i=i):
                out_share(v, i).wait_send()

    for chunk in range(lefts[-1]):
        pltpu.make_async_copy(done_part(0, 0, 0), out_place(chunk), o_recv.at[chunk]).wait()


def solution(mesh):
    R, C = mesh.shape["row"], mesh.shape["col"]
    NZ, NY = R // 2, C // 2
    axes = ("row", "col")

    def on_device(tokens, gate_weight, up_weight, tile_mask):
        depth, cols = gate_weight.shape
        row_tiles, col_tiles = depth // TILE, cols // TILE
        tiles = row_tiles * col_tiles
        slots = 5 * tiles // 8
        rows = tokens.shape[0]
        r = lax.axis_index("row")
        core = lax.axis_index("col") % 2
        home = ((r // 2) % 2) == core

        mask_sib = lax.ppermute(tile_mask, axes, [(d, d ^ 1) for d in range(R * C)])
        smem = pl.BlockSpec(memory_space=pltpu.SMEM)
        hbm = pl.BlockSpec(memory_space=pl.ANY)
        place = jnp.arange(tiles)
        place = (place % col_tiles) * row_tiles + place // col_tiles
        upto = (place[None, :] <= place[:, None]).astype(jnp.int32)

        def slot_codes(mask):
            mask = mask.reshape(R, tiles)
            return jnp.where(mask == 1, jnp.sum(mask[:, None, :] * upto[None], axis=2) - 1, -1)

        here = slot_codes(tile_mask)
        match = here[:, None, :] == jnp.arange(slots)[None, :, None]
        corner = jnp.stack([jnp.arange(tiles) // col_tiles, jnp.arange(tiles) % col_tiles])
        order = jnp.sum(jnp.where(match[None], corner[:, None, None, :], 0), axis=3).reshape(-1)
        codes = slot_codes(jnp.where(home, tile_mask, mask_sib)).reshape(-1)

        levels = levels_of(row_tiles, col_tiles, slots)
        L = len(levels)
        sizes = [stop - start for (stop, _), start in zip(levels, [0] + [v for v, _ in levels])]
        chunk_tiles = min(4, levels[0][1] // 2)
        width = chunk_tiles * TILE
        chunks = col_tiles // chunk_tiles
        most = (col_tiles - levels[-2][1]) // (2 * chunk_tiles)
        nc = len(parts_of(levels))
        bf16, f32 = jnp.bfloat16, jnp.float32
        pieces = [pltpu.VMEM((2, size, TILE, TILE), bf16) for size in sizes]
        for _ in range(2 * NZ):
            pieces += [pltpu.VMEM((size, TILE, TILE), bf16) for size in sizes]
        sem = pltpu.SemaphoreType.DMA
        hidden = pl.pallas_call(
            functools.partial(main_kernel, R, C, row_tiles, col_tiles, slots),
            out_shape=jax.ShapeDtypeStruct((rows, cols), bf16),
            in_specs=[smem, smem, hbm, hbm, hbm],
            out_specs=hbm,
            scratch_shapes=pieces + [
                pltpu.VMEM((2 * rows, tokens.shape[1] * C), bf16),
                pltpu.VMEM((chunks, 2 * rows, width), f32),
                pltpu.VMEM((depth, width), bf16),
                pltpu.VMEM((most, 2 * rows, width), f32),
                pltpu.VMEM((chunks // 2, 2 * rows, width), bf16),
                sem((nc,)), sem((nc,)), sem((2,)),
                sem((NZ, nc)), sem((NZ, nc)), sem((NZ, nc)), sem((NZ, nc)),
                sem, sem((2, NY)), sem((2, NY)), sem((2, NY)), sem((2, NY)),
                sem((L, most, 2)), sem((L, most, 2)), sem((chunks // 2,)), sem((chunks // 2,)),
                sem((chunks,)), pltpu.SemaphoreType.REGULAR,
            ],
            compiler_params=pltpu.CompilerParams(
                vmem_limit_bytes=VMEM_LIMIT, collective_id=0, has_side_effects=True),
            cost_estimate=pl.CostEstimate(
                flops=8 * rows * depth * R * cols // 2, bytes_accessed=rows * cols * 2, transcendentals=rows * cols),
            name="main",
        )(codes, order, tokens, gate_weight, up_weight)
        part = pl.BlockSpec((rows // 4, cols), lambda n: (n, 0))
        return pl.pallas_call(
            copy_kernel,
            out_shape=jax.ShapeDtypeStruct((rows, cols), bf16),
            grid=(4,),
            in_specs=[part],
            out_specs=part,
            name="place",
        )(hidden)

    placed = (P("row", "col"), P("row", "col"), P("row", "col"), P(None, "col"))
    return jax.shard_map(
        on_device, mesh=mesh, in_specs=placed, out_specs=P("row", "col"), check_vma=False
    )
```

```python
import functools

import jax
import jax.numpy as jnp
from jax import lax
from jax.experimental import pallas as pl
from jax.experimental.pallas import tpu as pltpu
from jax.sharding import PartitionSpec as P

TILE = 128
VMEM_LIMIT = 63 * 1024 * 1024
AHEAD, LAG = 4, 3
T1, T2, T3 = 0.5, 0.75, 1.0
MESH = pl.DeviceIdType.MESH


def copy_kernel(count, in_ref, out_ref, held, in_sem, out_sem):
    part = in_ref.shape[0] // count

    def read(n):
        return pltpu.make_async_copy(in_ref.at[pl.ds(n * part, part)], held.at[n], in_sem.at[n])

    def write(n):
        return pltpu.make_async_copy(held.at[n], out_ref.at[pl.ds(n * part, part)], out_sem.at[n])

    for n in range(count):
        read(n).start()
    for n in range(count):
        read(n).wait()
        write(n).start()
    for n in range(count):
        write(n).wait()


def split(total, parts):
    parts = min(parts, total)
    edges = [total * n // parts for n in range(parts + 1)]
    return [(a, b - a) for a, b in zip(edges, edges[1:])]


def levels_of(row_tiles, col_tiles, slots):
    cuts = [col_tiles // 4, col_tiles // 2] if col_tiles >= 8 else [col_tiles // 2]
    return [(row_tiles * cols, cols) for cols in cuts] + [(slots, col_tiles)]


def parts_of(levels):
    parts, start = [], 0
    for n, (stop, _) in enumerate(levels):
        parts += [(n, *v) for v in split(stop - start, 4)]
        start = stop
    return parts


def main_kernel(R, C, row_tiles, col_tiles, slots, codes_ref, order_ref, tok_in, gate_in, up_in, out_ref, *scratch):
    NZ, NY = R // 2, C // 2
    rows, wide = tok_in.shape
    depth = row_tiles * TILE
    levels = levels_of(row_tiles, col_tiles, slots)
    L = len(levels)
    bottoms = [0] + [stop for stop, _ in levels[:-1]]
    chunk_tiles = min(4, levels[0][1] // 2)
    width = chunk_tiles * TILE
    lefts = [0] + [cols // chunk_tiles for _, cols in levels]
    per_core = [(b - a) // 2 for a, b in zip(lefts, lefts[1:])]
    parts = parts_of(levels)
    nc = len(parts)
    at_level = [[n for n in range(nc) if parts[n][0] == v] for v in range(L)]

    scratch = list(scratch)
    take = lambda n: [scratch.pop(0) for _ in range(n)]
    own = take(L)
    other = take(L)
    far = [None] + [take(L) for _ in range(1, NZ)]
    across = [take(L) for _ in range(NZ)]
    tok, acc, dense, given, done = take(5)
    (w_send, w_recv, w_load, z_send, z_recv, x_send, x_recv, t_here, t_send, t_recv, ts_send, ts_recv,
     a_send, a_recv, o_send, os_send, o_recv, free) = take(18)

    r, c = lax.axis_index("row"), lax.axis_index("col")
    core = c % 2
    parity = (r // 2) % 2
    sibling = (r, c ^ 1)
    x_pair = (r ^ 1, c)
    owner = (c // 2) * 2 + parity

    def remote(src, dst, send, recv, device):
        return pltpu.make_async_remote_copy(
            src_ref=src, dst_ref=dst, send_sem=send, recv_sem=recv, device_id=device, device_id_type=MESH)

    def load(ref, n):
        return pltpu.make_async_copy(ref, tok.at[pl.ds(n * depth, depth), pl.ds(0, col_tiles * TILE)], w_load.at[n])

    @pl.when(core == 0)
    def _():
        load(up_in, 0).start()
        load(gate_in, 1).start()

    @pl.when(core == 1)
    def _():
        load(gate_in, 0).start()
        load(up_in, 1).start()

    for kind in range(2):
        load(gate_in, kind).wait()
    for kind in range(2):
        for v in range(L):
            def pack_step(s, carry, v=v, kind=kind):
                n = bottoms[v] + s
                i, j = order_ref[0, r, n], order_ref[1, r, n]
                tile = tok[pl.ds((kind * row_tiles + i) * TILE, TILE), pl.ds(j * TILE, TILE)]
                if kind:
                    own[v][core, s] = tile
                else:
                    other[v][s] = tile
                return carry

            count = levels[v][0] - bottoms[v]
            lax.fori_loop(0, count, pack_step, 0, unroll=min(4, count))

    partners = [sibling, x_pair, (r ^ 2, c ^ 1)]
    partners += [(r ^ (2 * d), c) for d in range(1, NZ)]
    partners += [(r, (c + 2 * s) % C) for s in range(1, NY)]
    barrier = pltpu.get_barrier_semaphore()
    for device in partners:
        pl.semaphore_signal(barrier, inc=1, device_id=device, device_id_type=MESH)
    pl.semaphore_wait(barrier, len(partners))

    def own_part(index, n):
        half, start, size = parts[n]
        return own[half].at[index, pl.ds(start, size)]

    def piece_part(piece, n):
        half, start, size = parts[n]
        return piece[half].at[pl.ds(start, size)]

    def w_copy(n):
        return remote(piece_part(other, n), own_part(core, n), w_send.at[n], w_recv.at[n], sibling)

    def w_arrival(n):
        return remote(piece_part(other, n), own_part(1 - core, n), w_send.at[n], w_recv.at[n], sibling)

    def z_copy(d, n):
        index = parity if d % 2 == 0 else 1 - parity
        return remote(own_part(index, n), piece_part(far[d], n), z_send.at[d, n], z_recv.at[d, n],
                      (r ^ (2 * d), c))

    def x_copy(d, n):
        src = own_part(parity, n) if d == 0 else piece_part(far[d], n)
        return remote(src, piece_part(across[d], n), x_send.at[d, n], x_recv.at[d, n], x_pair)

    def tok_place(group, col):
        return tok.at[pl.ds(group * rows, rows), pl.ds(pl.multiple_of(col * wide, TILE), wide)]

    def tok_copy(group, s):
        src = tok_in if group == 0 else tok_place(1, c)
        if s == 0:
            return remote(tok_in, tok_place(1, c), t_send.at[1, 0], t_recv.at[1, 0], (r ^ 2, c))
        return remote(src, tok_place(group, c), t_send.at[group, s], t_recv.at[group, s], (r, (c + 2 * s) % C))

    def tok_arrival(group, s):
        return remote(tok_in, tok_place(group, (c - 2 * s) % C), t_send.at[group, s], t_recv.at[group, s],
                      sibling)

    def tok_share(group, s):
        col = (c - 2 * s) % C
        src = tok_in if group == 0 and s == 0 else tok_place(group, col)
        return remote(src, tok_place(group, col), ts_send.at[group, s], ts_recv.at[group, s], sibling)

    def tok_shared(group, s):
        return remote(tok_in, tok_place(group, ((c ^ 1) - 2 * s) % C), ts_send.at[group, s],
                      ts_recv.at[group, s], sibling)

    tok_local = pltpu.make_async_copy(tok_in, tok_place(0, c), t_here)

    w_copy(0).start()
    tok_copy(1, 0).start()
    for n in range(1, nc):
        w_copy(n).start()
    for s in range(1, NY):
        tok_copy(0, s).start()
    cut = [d for d in range(2, NZ, 2)] + [d for d in range(3, NZ, 2)]
    order = [(d, n) for v in range(L) for d in cut for n in at_level[v]]
    ahead = AHEAD
    for n in range(nc):
        w_arrival(n).wait_recv()
        if n < ahead:
            z_copy(1, n).start()
            z_copy(*order[n]).start()
        x_copy(0, n).start()
    tok_share(0, 0).start()
    tok_local.start()

    def clear(n, carry):
        acc[n] = jnp.zeros(acc.shape[1:], acc.dtype)
        return carry

    lax.fori_loop(0, acc.shape[0], clear, 0)

    def job(piece, index, source, v, bounds):
        count, place, after = bounds

        def step(n, carry):
            chunk = place(n)
            for j in range(chunk_tiles):
                for i in range(row_tiles):
                    code = codes_ref[source, i * col_tiles + chunk * chunk_tiles + j]
                    value = None
                    for u in range(v + 1):
                        size = levels[u][0] - bottoms[u]
                        slot = jnp.minimum(jnp.maximum(code - bottoms[u], 0), size - 1)
                        tile = piece[u][slot] if index is None else piece[u][index, slot]
                        value = jnp.where(code >= bottoms[u], tile, jnp.zeros_like(tile) if value is None else value)
                    dense[pl.ds(i * TILE, TILE), pl.ds(j * TILE, TILE)] = value
            lhs = tok[:, pl.ds(pl.multiple_of(source * depth, TILE), depth)]
            acc[chunk] += jnp.dot(lhs, dense[...], preferred_element_type=jnp.float32)
            if after:
                after(n)
            return carry

        lax.fori_loop(0, count, step, 0)

    def our_chunk(v, i):
        return lefts[v] + core * per_core[v] + i

    def their_chunk(v, i):
        return lefts[v] + (1 - core) * per_core[v] + i

    def sums_copy(v, i, group):
        part = pl.ds(group * rows, rows)
        return remote(acc.at[their_chunk(v, i), part], given.at[i, part], a_send.at[v, i, group],
                      a_recv.at[v, i, group], sibling)

    every = [(2 * per_core[v], lambda n, v=v: lefts[v] + n, None) for v in range(L)]
    theirs = [(per_core[v], functools.partial(their_chunk, v), None) for v in range(L)]
    sent = [(per_core[v], functools.partial(their_chunk, v), lambda n, v=v: sums_copy(v, n, 1).start())
            for v in range(L)]
    ours = [(per_core[v], functools.partial(our_chunk, v), None) for v in range(L)]

    def near_job(d, v, bounds=every):
        if d == 0:
            job(own, parity, r, v, bounds[v])
        else:
            job(far[d], None, r ^ (2 * d), v, bounds[v])

    arrived = set()

    def across_job(d, v, bounds=every):
        for n in range(nc):
            if parts[n][0] <= v and (d, n) not in arrived:
                arrived.add((d, n))
                x_copy(d, n).wait_recv()
        job(across[d], None, r ^ (2 * d) ^ 1, v, bounds[v])

    def out_place(chunk):
        return out_ref.at[:, pl.ds(pl.multiple_of(chunk * width, TILE), width)]

    def done_part(v, i, group):
        return done.at[sum(per_core[:v]) + i, pl.ds(group * rows, rows)]

    def out_copy(v, i):
        return remote(done_part(v, i, 1), out_place(our_chunk(v, i)), o_send.at[sum(per_core[:v]) + i],
                      o_recv.at[our_chunk(v, i)], (r ^ 2, owner))

    def out_share(v, i):
        return remote(done_part(v, i, 0), out_place(our_chunk(v, i)), os_send.at[sum(per_core[:v]) + i],
                      o_recv.at[our_chunk(v, i)], sibling)

    def out_local(v, i):
        return pltpu.make_async_copy(done_part(v, i, 0), out_place(our_chunk(v, i)), o_recv.at[our_chunk(v, i)])

    def finish(v, i, group):
        sums_copy(v, i, group).wait_recv()
        chunk = our_chunk(v, i)
        block = min(128, rows)

        def rows_step(n, carry):
            here = pl.ds(pl.multiple_of(group * rows + n * block, block), block)
            a, b = acc[chunk, here], given[i, here]
            gate = jnp.where(core == 0, a, b)
            up = jnp.where(core == 0, b, a)
            done[sum(per_core[:v]) + i, here] = (gate / (1.0 + jnp.exp(-gate)) * up).astype(done.dtype)
            return carry

        lax.fori_loop(0, rows // block, rows_step, 0)
        if group:
            out_copy(v, i).start()
        else:
            @pl.when(core == parity)
            def _():
                out_local(v, i).start()

            @pl.when(core != parity)
            def _():
                out_share(v, i).start()

    state = dict(pair=0)
    later = []

    def pass_on(s):
        d, n = order[s]
        z_copy(d, n).wait_recv()
        x_copy(d, n).start()
        if s + ahead < len(order):
            z_copy(*order[s + ahead]).start()

    def pair_step():
        n = state["pair"]
        if n < nc:
            z_copy(1, n).wait_recv()
            if n in at_level[-1]:
                later.append((1, n))
            else:
                x_copy(1, n).start()
            if n + ahead < nc:
                z_copy(1, n + ahead).start()
            state["pair"] = n + 1

    def tokens_1():
        tok_arrival(1, 0).wait_recv()
        for s in range(1, NY):
            tok_copy(1, s).start()
        tok_share(1, 0).start()
        for s in range(1, NY):
            tok_arrival(0, s).wait_recv()
            tok_share(0, s).start()

    def tokens_2():
        for q in range(1, NY):
            tok_arrival(1, q).wait_recv()
            tok_share(1, q).start()

    def tokens_3():
        tok_local.wait()
        for g in range(2):
            for q in range(NY):
                tok_shared(g, q).wait_recv()

    steps = len(order)
    starts = [order.index((cut[0], at_level[v][0])) for v in range(L)]
    spread = starts[1] if L > 2 else starts[1] // 2
    head = len(at_level[0]) * len(cut)
    last = cut[-1]
    queue = []

    def at(step, cost, item):
        queue.append((max(step, 0), len(queue), cost, item))

    at(int(T1 * head) - 1, 0, tokens_1)
    at(int(T2 * head) - 1, 0, tokens_2)
    ready = int(T3 * head) - 1
    at(ready, 0, tokens_3)
    for v in range(L):
        there = {d: order.index((d, at_level[v][-1])) for d in cut}
        cost = 2 * per_core[v]
        at(max(ready, starts[max(v - 1, 0)]), cost, functools.partial(near_job, 0, v))
        at(max(ready, at_level[v][-1]), cost, functools.partial(near_job, 1, v))
        if v == L - 1:
            own_there = pair_there = starts[-1] + 1
        else:
            own_there = spread + at_level[v][-1] - at_level[1][0] + LAG if v else 0
            pair_there = at_level[v][-1] + LAG
        at(max(ready, own_there), cost, functools.partial(across_job, 0, v))
        at(max(ready, pair_there), cost, functools.partial(across_job, 1, v))
        for d in cut:
            final = v == L - 1 and d == last
            if not final:
                at(max(ready, there[d]), cost, functools.partial(near_job, d, v))
            if d != last:
                at(max(ready, there[d] + LAG), cost, functools.partial(across_job, d, v))

        def send_sums(v=v):
            if v:
                pl.semaphore_wait(free, 1)
            if v == L - 1:
                near_job(last, v, theirs)
            across_job(last, v, sent)
            if v == L - 1:
                near_job(last, v, ours)
            across_job(last, v, ours)
            for i in range(per_core[v]):
                sums_copy(v, i, 0).start()

        when = max(ready, there[last] + LAG) if v < L - 1 else steps
        at(when, cost, send_sums)
        for group in (1, 0):
            for i in range(per_core[v]):
                at(when + 1, 2, functools.partial(finish, v, i, group))

        def release(v=v):
            for group in range(2):
                for i in range(per_core[v]):
                    sums_copy(v, i, group).wait_send()
            if v < L - 1:
                pl.semaphore_signal(free, inc=1, device_id=sibling, device_id_type=MESH)

        at(when + 1, 0, release)

    queue.sort(key=lambda entry: entry[:2])
    for s in range(steps):
        pass_on(s)
        pair_step()
        if s >= spread:
            for _ in range(min(len(later), 1 if later and parts[later[0][1]][0] < L - 1 else 2)):
                x_copy(*later.pop(0)).start()
        if s + 1 == starts[-1]:
            while state["pair"] < nc:
                pair_step()
            while later:
                x_copy(*later.pop(0)).start()
        budget = 6 if s < starts[-1] else 4
        while queue and queue[0][0] <= s and budget > 0:
            _, _, cost, item = queue.pop(0)
            item()
            budget -= cost
    for entry in queue:
        entry[3]()

    for n in range(nc):
        w_copy(n).wait_send()
        for d in range(NZ):
            x_copy(d, n).wait_send()
            if d:
                z_copy(d, n).wait_send()
    for g in range(2):
        for s in range(NY):
            if g or s:
                tok_copy(g, s).wait_send()
            tok_share(g, s).wait_send()
    for v in range(L):
        for i in range(per_core[v]):
            out_copy(v, i).wait_send()

            @pl.when(core != parity)
            def _(v=v, i=i):
                out_share(v, i).wait_send()

    for chunk in range(lefts[-1]):
        pltpu.make_async_copy(done_part(0, 0, 0), out_place(chunk), o_recv.at[chunk]).wait()


def solution(mesh):
    R, C = mesh.shape["row"], mesh.shape["col"]
    NZ, NY = R // 2, C // 2
    axes = ("row", "col")

    def on_device(tokens, gate_weight, up_weight, tile_mask):
        depth, cols = gate_weight.shape
        row_tiles, col_tiles = depth // TILE, cols // TILE
        tiles = row_tiles * col_tiles
        slots = 5 * tiles // 8
        rows = tokens.shape[0]
        r = lax.axis_index("row")
        core = lax.axis_index("col") % 2
        home = ((r // 2) % 2) == core

        mask_sib = lax.ppermute(tile_mask, axes, [(d, d ^ 1) for d in range(R * C)])
        smem = pl.BlockSpec(memory_space=pltpu.SMEM)
        hbm = pl.BlockSpec(memory_space=pl.ANY)
        place = jnp.arange(tiles)
        place = (place % col_tiles) * row_tiles + place // col_tiles
        upto = (place[None, :] <= place[:, None]).astype(jnp.int32)

        def slot_codes(mask):
            mask = mask.reshape(R, tiles)
            return jnp.where(mask == 1, jnp.sum(mask[:, None, :] * upto[None], axis=2) - 1, -1)

        here = slot_codes(tile_mask)
        match = here[:, None, :] == jnp.arange(slots)[None, :, None]
        corner = jnp.stack([jnp.arange(tiles) // col_tiles, jnp.arange(tiles) % col_tiles])
        order = jnp.sum(jnp.where(match[None], corner[:, None, None, :], 0), axis=3)
        codes = slot_codes(jnp.where(home, tile_mask, mask_sib))

        levels = levels_of(row_tiles, col_tiles, slots)
        L = len(levels)
        sizes = [stop - start for (stop, _), start in zip(levels, [0] + [v for v, _ in levels])]
        chunk_tiles = min(4, levels[0][1] // 2)
        width = chunk_tiles * TILE
        chunks = col_tiles // chunk_tiles
        most = (col_tiles - levels[-2][1]) // (2 * chunk_tiles)
        nc = len(parts_of(levels))
        bf16, f32 = jnp.bfloat16, jnp.float32
        pieces = [pltpu.VMEM((2, size, TILE, TILE), bf16) for size in sizes]
        for _ in range(2 * NZ):
            pieces += [pltpu.VMEM((size, TILE, TILE), bf16) for size in sizes]
        sem = pltpu.SemaphoreType.DMA
        hidden = pl.pallas_call(
            functools.partial(main_kernel, R, C, row_tiles, col_tiles, slots),
            out_shape=jax.ShapeDtypeStruct((rows, cols), bf16),
            in_specs=[smem, smem, hbm, hbm, hbm],
            out_specs=hbm,
            scratch_shapes=pieces + [
                pltpu.VMEM((2 * rows, tokens.shape[1] * C), bf16),
                pltpu.VMEM((chunks, 2 * rows, width), f32),
                pltpu.VMEM((depth, width), bf16),
                pltpu.VMEM((most, 2 * rows, width), f32),
                pltpu.VMEM((chunks // 2, 2 * rows, width), bf16),
                sem((nc,)), sem((nc,)), sem((2,)),
                sem((NZ, nc)), sem((NZ, nc)), sem((NZ, nc)), sem((NZ, nc)),
                sem, sem((2, NY)), sem((2, NY)), sem((2, NY)), sem((2, NY)),
                sem((L, most, 2)), sem((L, most, 2)), sem((chunks // 2,)), sem((chunks // 2,)),
                sem((chunks,)), pltpu.SemaphoreType.REGULAR,
            ],
            compiler_params=pltpu.CompilerParams(
                vmem_limit_bytes=VMEM_LIMIT, collective_id=0, has_side_effects=True),
            cost_estimate=pl.CostEstimate(
                flops=8 * rows * depth * R * cols // 2, bytes_accessed=rows * cols * 2, transcendentals=rows * cols),
            name="main",
        )(codes, order, tokens, gate_weight, up_weight)
        count = 8
        return pl.pallas_call(
            functools.partial(copy_kernel, count),
            out_shape=jax.ShapeDtypeStruct((rows, cols), bf16),
            in_specs=[hbm],
            out_specs=hbm,
            scratch_shapes=[pltpu.VMEM((count, rows // count, cols), bf16), sem((count,)), sem((count,))],
            name="place",
        )(hidden)

    placed = (P("row", "col"), P("row", "col"), P("row", "col"), P(None, "col"))
    return jax.shard_map(
        on_device, mesh=mesh, in_specs=placed, out_specs=P("row", "col"), check_vma=False
    )
```

```python
import functools

import jax
import jax.numpy as jnp
from jax import lax
from jax.experimental import pallas as pl
from jax.experimental.pallas import tpu as pltpu
from jax.sharding import PartitionSpec as P

TILE = 128
VMEM_LIMIT = 63 * 1024 * 1024
AHEAD, LAG = 4, 3
T1, T2, T3 = 0.5, 0.75, 1.0
MESH = pl.DeviceIdType.MESH


def copy_kernel(count, in_ref, out_ref, held, in_sem, out_sem):
    part = in_ref.shape[0] // count

    def read(n):
        return pltpu.make_async_copy(in_ref.at[pl.ds(n * part, part)], held.at[n], in_sem.at[n])

    def write(n):
        return pltpu.make_async_copy(held.at[n], out_ref.at[pl.ds(n * part, part)], out_sem.at[n])

    for n in range(count):
        read(n).start()
    for n in range(count):
        read(n).wait()
        write(n).start()
    for n in range(count):
        write(n).wait()


def split(total, parts):
    parts = min(parts, total)
    edges = [total * n // parts for n in range(parts + 1)]
    return [(a, b - a) for a, b in zip(edges, edges[1:])]


def levels_of(row_tiles, col_tiles, slots):
    cuts = [col_tiles // 4, col_tiles // 2] if col_tiles >= 8 else [col_tiles // 2]
    return [(row_tiles * cols, cols) for cols in cuts] + [(slots, col_tiles)]


def parts_of(levels):
    parts, start = [], 0
    for n, (stop, _) in enumerate(levels):
        parts += [(n, *v) for v in split(stop - start, 4)]
        start = stop
    return parts


def main_kernel(R, C, row_tiles, col_tiles, slots, codes_ref, order_ref, tok_in, gate_in, up_in, out_ref, *scratch):
    NZ, NY = R // 2, C // 2
    rows, wide = tok_in.shape
    depth = row_tiles * TILE
    levels = levels_of(row_tiles, col_tiles, slots)
    L = len(levels)
    bottoms = [0] + [stop for stop, _ in levels[:-1]]
    chunk_tiles = min(4, levels[0][1] // 2)
    width = chunk_tiles * TILE
    lefts = [0] + [cols // chunk_tiles for _, cols in levels]
    per_core = [(b - a) // 2 for a, b in zip(lefts, lefts[1:])]
    parts = parts_of(levels)
    nc = len(parts)
    at_level = [[n for n in range(nc) if parts[n][0] == v] for v in range(L)]

    scratch = list(scratch)
    take = lambda n: [scratch.pop(0) for _ in range(n)]
    own = take(L)
    other = take(L)
    far = [None] + [take(L) for _ in range(1, NZ)]
    across = [take(L) for _ in range(NZ)]
    tok, acc, dense, given, done = take(5)
    (w_send, w_recv, w_load, z_send, z_recv, x_send, x_recv, t_here, t_send, t_recv, ts_send, ts_recv,
     a_send, a_recv, o_send, os_send, o_recv, free) = take(18)

    r, c = lax.axis_index("row"), lax.axis_index("col")
    core = c % 2
    parity = (r // 2) % 2
    sibling = (r, c ^ 1)
    x_pair = (r ^ 1, c)
    owner = (c // 2) * 2 + parity

    def remote(src, dst, send, recv, device):
        return pltpu.make_async_remote_copy(
            src_ref=src, dst_ref=dst, send_sem=send, recv_sem=recv, device_id=device, device_id_type=MESH)

    def load(ref, n):
        return pltpu.make_async_copy(ref, tok.at[pl.ds(n * depth, depth), pl.ds(0, col_tiles * TILE)], w_load.at[n])

    @pl.when(core == 0)
    def _():
        load(up_in, 0).start()
        load(gate_in, 1).start()

    @pl.when(core == 1)
    def _():
        load(gate_in, 0).start()
        load(up_in, 1).start()

    for kind in range(2):
        load(gate_in, kind).wait()
    for kind in range(2):
        for v in range(L):
            def pack_step(s, carry, v=v, kind=kind):
                n = bottoms[v] + s
                i, j = order_ref[0, r, n], order_ref[1, r, n]
                tile = tok[pl.ds((kind * row_tiles + i) * TILE, TILE), pl.ds(j * TILE, TILE)]
                if kind:
                    own[v][core, s] = tile
                else:
                    other[v][s] = tile
                return carry

            count = levels[v][0] - bottoms[v]
            lax.fori_loop(0, count, pack_step, 0, unroll=min(4, count))

    partners = [sibling, x_pair, (r ^ 2, c ^ 1)]
    partners += [(r ^ (2 * d), c) for d in range(1, NZ)]
    partners += [(r, (c + 2 * s) % C) for s in range(1, NY)]
    barrier = pltpu.get_barrier_semaphore()
    for device in partners:
        pl.semaphore_signal(barrier, inc=1, device_id=device, device_id_type=MESH)
    pl.semaphore_wait(barrier, len(partners))

    def own_part(index, n):
        half, start, size = parts[n]
        return own[half].at[index, pl.ds(start, size)]

    def piece_part(piece, n):
        half, start, size = parts[n]
        return piece[half].at[pl.ds(start, size)]

    def w_copy(n):
        return remote(piece_part(other, n), own_part(core, n), w_send.at[n], w_recv.at[n], sibling)

    def w_arrival(n):
        return remote(piece_part(other, n), own_part(1 - core, n), w_send.at[n], w_recv.at[n], sibling)

    def z_copy(d, n):
        index = parity if d % 2 == 0 else 1 - parity
        return remote(own_part(index, n), piece_part(far[d], n), z_send.at[d, n], z_recv.at[d, n],
                      (r ^ (2 * d), c))

    def x_copy(d, n):
        src = own_part(parity, n) if d == 0 else piece_part(far[d], n)
        return remote(src, piece_part(across[d], n), x_send.at[d, n], x_recv.at[d, n], x_pair)

    def tok_place(group, col):
        return tok.at[pl.ds(group * rows, rows), pl.ds(pl.multiple_of(col * wide, TILE), wide)]

    def tok_copy(group, s):
        src = tok_in if group == 0 else tok_place(1, c)
        if s == 0:
            return remote(tok_in, tok_place(1, c), t_send.at[1, 0], t_recv.at[1, 0], (r ^ 2, c))
        return remote(src, tok_place(group, c), t_send.at[group, s], t_recv.at[group, s], (r, (c + 2 * s) % C))

    def tok_arrival(group, s):
        return remote(tok_in, tok_place(group, (c - 2 * s) % C), t_send.at[group, s], t_recv.at[group, s],
                      sibling)

    def tok_share(group, s):
        col = (c - 2 * s) % C
        src = tok_in if group == 0 and s == 0 else tok_place(group, col)
        return remote(src, tok_place(group, col), ts_send.at[group, s], ts_recv.at[group, s], sibling)

    def tok_shared(group, s):
        return remote(tok_in, tok_place(group, ((c ^ 1) - 2 * s) % C), ts_send.at[group, s],
                      ts_recv.at[group, s], sibling)

    tok_local = pltpu.make_async_copy(tok_in, tok_place(0, c), t_here)

    w_copy(0).start()
    tok_copy(1, 0).start()
    for n in range(1, nc):
        w_copy(n).start()
    for s in range(1, NY):
        tok_copy(0, s).start()
    cut = [d for d in range(3, NZ, 2)] + [d for d in range(2, NZ, 2)]
    order = [(d, n) for v in range(L) for d in cut for n in at_level[v]]
    ahead = AHEAD
    for n in range(nc):
        w_arrival(n).wait_recv()
        if n < ahead:
            z_copy(1, n).start()
            z_copy(*order[n]).start()
        x_copy(0, n).start()
    tok_share(0, 0).start()
    tok_local.start()

    def clear(n, carry):
        acc[n] = jnp.zeros(acc.shape[1:], acc.dtype)
        return carry

    lax.fori_loop(0, acc.shape[0], clear, 0)

    def job(piece, index, source, v, bounds):
        count, place, after = bounds

        def step(n, carry):
            chunk = place(n)
            for j in range(chunk_tiles):
                for i in range(row_tiles):
                    code = codes_ref[source, i * col_tiles + chunk * chunk_tiles + j]
                    value = None
                    for u in range(v + 1):
                        size = levels[u][0] - bottoms[u]
                        slot = jnp.minimum(jnp.maximum(code - bottoms[u], 0), size - 1)
                        tile = piece[u][slot] if index is None else piece[u][index, slot]
                        value = jnp.where(code >= bottoms[u], tile, jnp.zeros_like(tile) if value is None else value)
                    dense[pl.ds(i * TILE, TILE), pl.ds(j * TILE, TILE)] = value
            lhs = tok[:, pl.ds(pl.multiple_of(source * depth, TILE), depth)]
            acc[chunk] += jnp.dot(lhs, dense[...], preferred_element_type=jnp.float32)
            if after:
                after(n)
            return carry

        lax.fori_loop(0, count, step, 0)

    def our_chunk(v, i):
        return lefts[v] + core * per_core[v] + i

    def their_chunk(v, i):
        return lefts[v] + (1 - core) * per_core[v] + i

    def sums_copy(v, i, group):
        part = pl.ds(group * rows, rows)
        return remote(acc.at[their_chunk(v, i), part], given.at[i, part], a_send.at[v, i, group],
                      a_recv.at[v, i, group], sibling)

    every = [(2 * per_core[v], lambda n, v=v: lefts[v] + n, None) for v in range(L)]
    theirs = [(per_core[v], functools.partial(their_chunk, v), None) for v in range(L)]
    sent = [(per_core[v], functools.partial(their_chunk, v), lambda n, v=v: sums_copy(v, n, 1).start())
            for v in range(L)]
    ours = [(per_core[v], functools.partial(our_chunk, v), None) for v in range(L)]

    def near_job(d, v, bounds=every):
        if d == 0:
            job(own, parity, r, v, bounds[v])
        else:
            job(far[d], None, r ^ (2 * d), v, bounds[v])

    arrived = set()

    def across_job(d, v, bounds=every):
        for n in range(nc):
            if parts[n][0] <= v and (d, n) not in arrived:
                arrived.add((d, n))
                x_copy(d, n).wait_recv()
        job(across[d], None, r ^ (2 * d) ^ 1, v, bounds[v])

    def out_place(chunk):
        return out_ref.at[:, pl.ds(pl.multiple_of(chunk * width, TILE), width)]

    def done_part(v, i, group):
        return done.at[sum(per_core[:v]) + i, pl.ds(group * rows, rows)]

    def out_copy(v, i):
        return remote(done_part(v, i, 1), out_place(our_chunk(v, i)), o_send.at[sum(per_core[:v]) + i],
                      o_recv.at[our_chunk(v, i)], (r ^ 2, owner))

    def out_share(v, i):
        return remote(done_part(v, i, 0), out_place(our_chunk(v, i)), os_send.at[sum(per_core[:v]) + i],
                      o_recv.at[our_chunk(v, i)], sibling)

    def out_local(v, i):
        return pltpu.make_async_copy(done_part(v, i, 0), out_place(our_chunk(v, i)), o_recv.at[our_chunk(v, i)])

    def finish(v, i, group):
        sums_copy(v, i, group).wait_recv()
        chunk = our_chunk(v, i)
        block = min(128, rows)

        def rows_step(n, carry):
            here = pl.ds(pl.multiple_of(group * rows + n * block, block), block)
            a, b = acc[chunk, here], given[i, here]
            gate = jnp.where(core == 0, a, b)
            up = jnp.where(core == 0, b, a)
            done[sum(per_core[:v]) + i, here] = (gate / (1.0 + jnp.exp(-gate)) * up).astype(done.dtype)
            return carry

        lax.fori_loop(0, rows // block, rows_step, 0)
        if group:
            out_copy(v, i).start()
        else:
            @pl.when(core == parity)
            def _():
                out_local(v, i).start()

            @pl.when(core != parity)
            def _():
                out_share(v, i).start()

    state = dict(pair=0)
    later = []

    def pass_on(s):
        d, n = order[s]
        z_copy(d, n).wait_recv()
        x_copy(d, n).start()
        if s + ahead < len(order):
            z_copy(*order[s + ahead]).start()

    def pair_step():
        n = state["pair"]
        if n < nc:
            z_copy(1, n).wait_recv()
            if n in at_level[-1]:
                later.append((1, n))
            else:
                x_copy(1, n).start()
            if n + ahead < nc:
                z_copy(1, n + ahead).start()
            state["pair"] = n + 1

    def tokens_1():
        tok_arrival(1, 0).wait_recv()
        for s in range(1, NY):
            tok_copy(1, s).start()
        tok_share(1, 0).start()
        for s in range(1, NY):
            tok_arrival(0, s).wait_recv()
            tok_share(0, s).start()

    def tokens_2():
        for q in range(1, NY):
            tok_arrival(1, q).wait_recv()
            tok_share(1, q).start()

    def tokens_3():
        tok_local.wait()
        for g in range(2):
            for q in range(NY):
                tok_shared(g, q).wait_recv()

    steps = len(order)
    starts = [order.index((cut[0], at_level[v][0])) for v in range(L)]
    spread = starts[1] if L > 2 else starts[1] // 2
    head = len(at_level[0]) * len(cut)
    last = cut[-1]
    queue = []

    def at(step, cost, item):
        queue.append((max(step, 0), len(queue), cost, item))

    at(int(T1 * head) - 1, 0, tokens_1)
    at(int(T2 * head) - 1, 0, tokens_2)
    ready = int(T3 * head) - 1
    at(ready, 0, tokens_3)
    for v in range(L):
        there = {d: order.index((d, at_level[v][-1])) for d in cut}
        cost = 2 * per_core[v]
        at(max(ready, starts[max(v - 1, 0)]), cost, functools.partial(near_job, 0, v))
        at(max(ready, at_level[v][-1]), cost, functools.partial(near_job, 1, v))
        if v == L - 1:
            own_there = pair_there = starts[-1] + 1
        else:
            own_there = spread + at_level[v][-1] - at_level[1][0] + LAG if v else 0
            pair_there = at_level[v][-1] + LAG
        at(max(ready, own_there), cost, functools.partial(across_job, 0, v))
        at(max(ready, pair_there), cost, functools.partial(across_job, 1, v))
        for d in cut:
            final = v == L - 1 and d == last
            if not final:
                at(max(ready, there[d]), cost, functools.partial(near_job, d, v))
            if d != last:
                at(max(ready, there[d] + LAG), cost, functools.partial(across_job, d, v))

        def send_sums(v=v):
            if v:
                pl.semaphore_wait(free, 1)
            if v == L - 1:
                near_job(last, v, theirs)
            across_job(last, v, sent)
            if v == L - 1:
                near_job(last, v, ours)
            across_job(last, v, ours)
            for i in range(per_core[v]):
                sums_copy(v, i, 0).start()

        when = max(ready, there[last] + LAG) if v < L - 1 else steps
        at(when, cost, send_sums)
        for group in (1, 0):
            for i in range(per_core[v]):
                at(when + 1, 2, functools.partial(finish, v, i, group))

        def release(v=v):
            for group in range(2):
                for i in range(per_core[v]):
                    sums_copy(v, i, group).wait_send()
            if v < L - 1:
                pl.semaphore_signal(free, inc=1, device_id=sibling, device_id_type=MESH)

        at(when + 1, 0, release)

    queue.sort(key=lambda entry: entry[:2])
    for s in range(steps):
        pass_on(s)
        pair_step()
        if s >= spread:
            for _ in range(min(len(later), 1 if later and parts[later[0][1]][0] < L - 1 else 2)):
                x_copy(*later.pop(0)).start()
        if s + 1 == starts[-1]:
            while state["pair"] < nc:
                pair_step()
            while later:
                x_copy(*later.pop(0)).start()
        budget = 6 if s < starts[-1] else 4
        while queue and queue[0][0] <= s and budget > 0:
            _, _, cost, item = queue.pop(0)
            item()
            budget -= cost
    for entry in queue:
        entry[3]()

    for n in range(nc):
        w_copy(n).wait_send()
        for d in range(NZ):
            x_copy(d, n).wait_send()
            if d:
                z_copy(d, n).wait_send()
    for g in range(2):
        for s in range(NY):
            if g or s:
                tok_copy(g, s).wait_send()
            tok_share(g, s).wait_send()
    for v in range(L):
        for i in range(per_core[v]):
            out_copy(v, i).wait_send()

            @pl.when(core != parity)
            def _(v=v, i=i):
                out_share(v, i).wait_send()

    for chunk in range(lefts[-1]):
        pltpu.make_async_copy(done_part(0, 0, 0), out_place(chunk), o_recv.at[chunk]).wait()


def solution(mesh):
    R, C = mesh.shape["row"], mesh.shape["col"]
    NZ, NY = R // 2, C // 2
    axes = ("row", "col")

    def on_device(tokens, gate_weight, up_weight, tile_mask):
        depth, cols = gate_weight.shape
        row_tiles, col_tiles = depth // TILE, cols // TILE
        tiles = row_tiles * col_tiles
        slots = 5 * tiles // 8
        rows = tokens.shape[0]
        r = lax.axis_index("row")
        core = lax.axis_index("col") % 2
        home = ((r // 2) % 2) == core

        mask_sib = lax.ppermute(tile_mask, axes, [(d, d ^ 1) for d in range(R * C)])
        smem = pl.BlockSpec(memory_space=pltpu.SMEM)
        hbm = pl.BlockSpec(memory_space=pl.ANY)
        place = jnp.arange(tiles)
        place = (place % col_tiles) * row_tiles + place // col_tiles
        upto = (place[None, :] <= place[:, None]).astype(jnp.int32)

        def slot_codes(mask):
            mask = mask.reshape(R, tiles)
            return jnp.where(mask == 1, jnp.sum(mask[:, None, :] * upto[None], axis=2) - 1, -1)

        here = slot_codes(tile_mask)
        match = here[:, None, :] == jnp.arange(slots)[None, :, None]
        corner = jnp.stack([jnp.arange(tiles) // col_tiles, jnp.arange(tiles) % col_tiles])
        order = jnp.sum(jnp.where(match[None], corner[:, None, None, :], 0), axis=3)
        codes = slot_codes(jnp.where(home, tile_mask, mask_sib))

        levels = levels_of(row_tiles, col_tiles, slots)
        L = len(levels)
        sizes = [stop - start for (stop, _), start in zip(levels, [0] + [v for v, _ in levels])]
        chunk_tiles = min(4, levels[0][1] // 2)
        width = chunk_tiles * TILE
        chunks = col_tiles // chunk_tiles
        most = (col_tiles - levels[-2][1]) // (2 * chunk_tiles)
        nc = len(parts_of(levels))
        bf16, f32 = jnp.bfloat16, jnp.float32
        pieces = [pltpu.VMEM((2, size, TILE, TILE), bf16) for size in sizes]
        for _ in range(2 * NZ):
            pieces += [pltpu.VMEM((size, TILE, TILE), bf16) for size in sizes]
        sem = pltpu.SemaphoreType.DMA
        hidden = pl.pallas_call(
            functools.partial(main_kernel, R, C, row_tiles, col_tiles, slots),
            out_shape=jax.ShapeDtypeStruct((rows, cols), bf16),
            in_specs=[smem, smem, hbm, hbm, hbm],
            out_specs=hbm,
            scratch_shapes=pieces + [
                pltpu.VMEM((2 * rows, tokens.shape[1] * C), bf16),
                pltpu.VMEM((chunks, 2 * rows, width), f32),
                pltpu.VMEM((depth, width), bf16),
                pltpu.VMEM((most, 2 * rows, width), f32),
                pltpu.VMEM((chunks // 2, 2 * rows, width), bf16),
                sem((nc,)), sem((nc,)), sem((2,)),
                sem((NZ, nc)), sem((NZ, nc)), sem((NZ, nc)), sem((NZ, nc)),
                sem, sem((2, NY)), sem((2, NY)), sem((2, NY)), sem((2, NY)),
                sem((L, most, 2)), sem((L, most, 2)), sem((chunks // 2,)), sem((chunks // 2,)),
                sem((chunks,)), pltpu.SemaphoreType.REGULAR,
            ],
            compiler_params=pltpu.CompilerParams(
                vmem_limit_bytes=VMEM_LIMIT, collective_id=0, has_side_effects=True),
            cost_estimate=pl.CostEstimate(
                flops=8 * rows * depth * R * cols // 2, bytes_accessed=rows * cols * 2, transcendentals=rows * cols),
            name="main",
        )(codes, order, tokens, gate_weight, up_weight)
        count = 8
        return pl.pallas_call(
            functools.partial(copy_kernel, count),
            out_shape=jax.ShapeDtypeStruct((rows, cols), bf16),
            in_specs=[hbm],
            out_specs=hbm,
            scratch_shapes=[pltpu.VMEM((count, rows // count, cols), bf16), sem((count,)), sem((count,))],
            name="place",
        )(hidden)

    placed = (P("row", "col"), P("row", "col"), P("row", "col"), P(None, "col"))
    return jax.shard_map(
        on_device, mesh=mesh, in_specs=placed, out_specs=P("row", "col"), check_vma=False
    )
```
